128 devices in a mesh: row: 8 (over z, y_hi), col: 16 (over y_lo, x, core).
Axes of the slice: x: 4, y: 4 (y_hi: 2, y_lo: 2; y = y_hi * 2 + y_lo), z: 4, core: 2. Of those that a mesh axis runs over, the one named last changes fastest.
Arguments:
- img_learner: bfloat16 [16384, 1152], P(('row', 'col')), may hold values from -0.30859375 to 0.30859375
- txt_learner: bfloat16 [16384, 1152], P(('col', 'row')), may hold values from -0.30859375 to 0.30859375
- img_ref: bfloat16 [16384, 1152], P(('row', 'col')), may hold values from -0.30859375 to 0.30859375
- txt_ref: bfloat16 [16384, 1152], P(('col', 'row')), may hold values from -0.30859375 to 0.30859375
- partner: int32 [16384], P(('row', 'col')), may hold values from 0 to 16383, each once
- synthetic: int32 [16384], P(('row', 'col')), may hold values 0 or 1
- span_ids: int32 [16384], P(('row', 'col')), may hold values from 0 to 63, as said below
Outputs:
- img_grad: bfloat16 [16384, 1152], P(('row', 'col'))
- txt_grad: bfloat16 [16384, 1152], P(('col', 'row'))
- span_weight: float32 [64], replicated
The draws below stay inside these ranges and needn't reach their ends.
Inputs may be any that keep to these rules, and one draw needn't show every extreme that they name: `span_ids`: every group holds exactly 256 images.
All inputs are finite; a program needn't handle non-finite values. No bound on the sum of `synthetic` on one device may be relied on, other than what follows from the above.
Results may differ from the reference program's by a relative error of at most 0.02.
Values may be sent and summed in bfloat16 or wider, within the bound.
No kernel may reach another device: no remote copies, remote signals or barrier semaphores. Data moves between devices by JAX's collectives and lax.ppermute only.
A program may use at most 64 MiB of HBM per device.

```python
import jax
import jax.numpy as jnp
from jax import lax

D = 1152
SPANS = 64
PAIRS = 16384
N_ROW = 8
N_COL = 16


def draw_span_ids(key, part):
    key = jax.random.fold_in(key, 7)
    order = jax.random.permutation(key, PAIRS)
    return (order % SPANS).astype(jnp.int32)


def touch_ends(entries, stream_key, least, top_value):
    extent = entries.shape
    place = [jax.random.randint(jax.random.fold_in(stream_key, axis), (), 0, extent[axis]) for axis in range(len(extent))]
    entries = entries.at[tuple(place)].set(least)
    longest = extent.index(max(extent))
    place[longest] = (place[longest] + 1) % extent[longest]
    return entries.at[tuple(place)].set(top_value)


def steps_of(stream_key, extent, split, low, top_value):
    level = 1.0
    for dim, shards_of in split:
        heights = jax.random.uniform(jax.random.fold_in(jax.random.fold_in(stream_key, 6), dim), (shards_of,), jnp.float32, low / len(split), top_value / len(split))
        level = level * jnp.repeat(jnp.exp(heights), extent[dim] // shards_of).reshape((-1,) + (1,) * (len(extent) - 1 - dim))
    return level


def centred(stream_key, extent, spread, limit, pieces=(), kind=jnp.bfloat16):
    gain = steps_of(stream_key, extent, pieces, -0.22, 0.18) if pieces else 1.0
    result = jax.random.normal(stream_key, extent, jnp.float32) * spread * gain
    return jnp.minimum(jnp.maximum(result, -limit), limit).astype(kind)


def setup_inputs(seed: int = 0) -> dict:
    key_of = jax.random.split(jax.random.key(seed), 8)
    return {
        "img_learner": centred(key_of[0], (PAIRS, D), (0.3 * D ** -0.25), 0.30859375, ((0, 128),)),
        "txt_learner": centred(key_of[1], (PAIRS, D), (0.3 * D ** -0.25), 0.30859375, ((0, 128),)),
        "img_ref": centred(key_of[2], (PAIRS, D), (0.3 * D ** -0.25), 0.30859375, ((0, 128),)),
        "txt_ref": centred(key_of[3], (PAIRS, D), (0.3 * D ** -0.25), 0.30859375, ((0, 128),)),
        "partner": jax.random.permutation(key_of[4], PAIRS).astype(jnp.int32),
        "synthetic": touch_ends((jax.random.randint(key_of[5], (PAIRS,), 0, 2) < 1).astype(jnp.int32), jax.random.fold_in(key_of[5], 1), 0, 1),
        "span_ids": draw_span_ids(jax.random.fold_in(key_of[7], 71), 0),
    }


scale_logit = 10.0
shift_logit = -5.0
sharpness = 5.0
synth_factor = 0.5


def logit_block(left, right):
    product = lax.dot_general(left, right, (((1,), (1,)), ((), ())), preferred_element_type=jnp.float32)
    return scale_logit * product + shift_logit


def reference(img_learner, txt_learner, img_ref, txt_ref, partner, synthetic, span_ids):
    row_count = PAIRS // N_ROW
    col_count = PAIRS // N_COL
    column_ids = jnp.arange(PAIRS, dtype=jnp.int32)
    span_table = (span_ids[:, None] == jnp.arange(SPANS, dtype=jnp.int32)[None, :]).astype(jnp.float32)

    def sign_block(index):
        owned = lax.dynamic_slice_in_dim(partner, index * row_count, row_count, 0)
        return jnp.where(owned[:, None] == column_ids[None, :], 1.0, -1.0).astype(jnp.float32)

    def excess_rows(index):
        start = index * row_count
        signed = sign_block(index)
        learner = logit_block(lax.dynamic_slice_in_dim(img_learner, start, row_count, 0), txt_learner)
        refer = logit_block(lax.dynamic_slice_in_dim(img_ref, start, row_count, 0), txt_ref)
        return jnp.sum(jax.nn.softplus(-signed * learner) - jax.nn.softplus(-signed * refer), axis=1)

    excess = lax.map(excess_rows, jnp.arange(N_ROW, dtype=jnp.int32)).reshape(PAIRS)
    score = jnp.dot(excess, span_table, precision=lax.Precision.HIGHEST)
    span_weight = jax.nn.sigmoid(sharpness * score / (PAIRS // SPANS))
    row_weight = jnp.dot(span_table, span_weight, precision=lax.Precision.HIGHEST)
    row_weight = row_weight * jnp.where(synthetic == 1, synth_factor, 1.0)
    text_groups = txt_learner.astype(jnp.float32).reshape(N_COL, col_count, D)

    def grad_rows(carry, index):
        start = index * row_count
        signed = sign_block(index)
        images = lax.dynamic_slice_in_dim(img_learner, start, row_count, 0)
        learner = logit_block(images, txt_learner)
        weights = lax.dynamic_slice_in_dim(row_weight, start, row_count, 0)
        grad_logit = (scale_logit * weights[:, None] * (-signed * jax.nn.sigmoid(-signed * learner))).astype(jnp.bfloat16)
        grouped = grad_logit.astype(jnp.float32).reshape(row_count, N_COL, col_count)
        partials = jnp.einsum("rnc,ncd->nrd", grouped, text_groups).astype(jnp.bfloat16)
        image_part = jnp.sum(partials.astype(jnp.float32), axis=0).astype(jnp.bfloat16)
        text_part = lax.dot_general(grad_logit, images, (((0,), (0,)), ((), ())), preferred_element_type=jnp.float32)
        carry = carry + text_part.astype(jnp.bfloat16).astype(jnp.float32)
        return carry, image_part

    text_sum, image_parts = lax.scan(grad_rows, jnp.zeros((PAIRS, D), jnp.float32), jnp.arange(N_ROW, dtype=jnp.int32))
    img_grad = image_parts.reshape(PAIRS, D)
    txt_grad = text_sum.astype(jnp.bfloat16)
    return img_grad, txt_grad, span_weight
```

```python
import functools

import jax
import jax.numpy as jnp
from jax import lax
from jax.experimental import pallas as pl
from jax.experimental.pallas import tpu as pltpu
from jax.sharding import PartitionSpec as P

SPANS = 64
D = 1152
SH = 128
CH = 2 * SH
NT = 8 * SH
NI = 8 * CH
META = 16
GROUP = 256.0
SCALE = 10.0
SHIFT = -5.0
SHARP = 5.0
SYNTH = 0.5
LN2 = 0.6931471805599453
LOG2E = 1.4426950408889634
AXES = ("row", "col")
F32 = jnp.float32
BF16 = jnp.bfloat16
MIB = 1 << 20

FLIPS = ("", "x", "y", "z", "xy", "yz", "zx", "xyz")


def place(index):
    row, col = divmod(index, 16)
    return dict(z=row // 2, y=2 * (row % 2) + col // 8, x=(col // 2) % 4, c=col % 2)


def device(z, y, x, c):
    return (2 * z + y // 2) * 16 + 8 * (y % 2) + 2 * x + c


def pairs(axis, kind):
    out = []
    for index in range(128):
        at = place(index)
        if axis == "c":
            at["c"] ^= 1
        else:
            k = at["c"] if kind == "mixed" else kind
            at[axis] = at[axis] ^ 1 if k == 0 else 3 - at[axis]
        out.append((index, device(**at)))
    return out


SWAP = {(a, k): pairs(a, k) for a in "xyz" for k in (0, 1, "mixed")}
SWAP["c"] = pairs("c", 0)


def swap(value, axis, kind=0):
    return lax.ppermute(value, AXES, SWAP["c"] if axis == "c" else SWAP[axis, kind])


def params(mib):
    return pltpu.CompilerParams(vmem_limit_bytes=mib * MIB)


def core_index():
    return lax.rem(lax.axis_index("col"), 2)


def payload_kernel(img, txt, img_other, txt_other, *rest):
    *meta, out = rest
    core = core_index()

    @pl.when(core == 0)
    def _():
        out[0:SH] = img[...]
        out[SH:CH] = img_other[...]

    @pl.when(core == 1)
    def _():
        out[0:SH] = txt_other[...]
        out[SH:CH] = txt[...]

    if meta:
        out[CH:] = jnp.zeros((META, D), BF16)
        row = lax.broadcasted_iota(jnp.int32, (META, SH), 0)
        for side, ref in enumerate(meta):
            partner, synth, span = (ref[i : i + 1, :] for i in range(3))
            high = lax.shift_right_logical(partner, 7)
            low = partner & 127
            block = jnp.where(row == 0, high, 0)
            block = jnp.where(row == 1, low, block)
            block = jnp.where(row == 2, span, block)
            block = jnp.where(row == 3, synth, block)
            out[CH:, side * SH : (side + 1) * SH] = block.astype(F32).astype(BF16)


def payload(img, txt, meta=None):
    others = [swap(img, "c"), swap(txt, "c")]
    metas = []
    if meta is not None:
        metas = [meta, swap(meta, "c")]
    rows = CH + (META if metas else 0)
    return pl.pallas_call(
        payload_kernel,
        out_shape=jax.ShapeDtypeStruct((rows, D), BF16),
        compiler_params=params(8),
        cost_estimate=pl.CostEstimate(flops=0, bytes_accessed=1 << 21, transcendentals=0),
    )(img, txt, *others, *metas)


def cube_gather(own, last):
    X, Y, Z = (swap(own, a, "mixed") for a in "xyz")
    XY, YZ, ZX = swap(Y, "x", "mixed"), swap(Z, "y", "mixed"), swap(X, "z", "mixed")
    XYZ = swap(YZ, "x", "mixed") if last == "x" else swap(ZX, "y", "mixed")
    return [own, X, Y, Z, XY, YZ, ZX, XYZ]


def text_base(k, core):
    row, col = lax.axis_index("row"), lax.axis_index("col")
    z, yh = row // 2, lax.rem(row, 2)
    yl, x = col // 8, lax.rem(col // 2, 4)
    y = 2 * yh + yl
    x = 3 - x if "x" in FLIPS[k] else x
    y = 3 - y if "y" in FLIPS[k] else y
    z = 3 - z if "z" in FLIPS[k] else z
    col = 8 * lax.rem(y, 2) + 2 * x + core
    row = 2 * z + y // 2
    return (col * 8 + row) * SH


def fetch(core, gs, ds, img, txt, sems, ks):
    waits = {}

    def one(name, sem, pick, dst, when_g):
        @pl.when(core == when_g)
        def _():
            pltpu.make_async_copy(pick(gs), dst, sem).start()

        @pl.when(core != when_g)
        def _():
            pltpu.make_async_copy(pick(ds), dst, sem).start()

        waits[name] = pltpu.make_async_copy(pick(gs), dst, sem)

    for k in ks:
        rows = pl.ds(pl.multiple_of(core * SH, SH), SH)
        one(("t", k), sems.at[k, 0], lambda r, k=k: r[k].at[rows], txt.at[k * SH : (k + 1) * SH], 1)
    for k in ks:
        for h in range(2):
            side = core if h == 0 else 1 - core
            rows = pl.ds(pl.multiple_of(side * SH, SH), SH)
            dst = img.at[h, k * SH : (k + 1) * SH]
            one(("i", k, h), sems.at[k, 1 + h], lambda r, k=k, rows=rows: r[k].at[rows], dst, 0)
    return waits


def fetch_meta(core, gs, ds, meta, sems, ks):
    waits = []
    for k in ks:

        @pl.when(core == 0)
        def _():
            pltpu.make_async_copy(gs[k].at[CH:, 0:CH], meta.at[k], sems.at[k, 3]).start()

        @pl.when(core != 0)
        def _():
            pltpu.make_async_copy(ds[k].at[CH:, 0:CH], meta.at[k], sems.at[k, 3]).start()

        waits.append(pltpu.make_async_copy(gs[k].at[CH:, 0:CH], meta.at[k], sems.at[k, 3]))
    return waits


def lanes(k, h):
    return slice(h * NT + k * SH, h * NT + (k + 1) * SH)


def spread_meta(core, meta, out, ks):
    for k in ks:
        block = meta[k].astype(F32)[0:8]
        low, high = block[:, 0:SH], block[:, SH:CH]
        out[:, lanes(k, 0)] = jnp.where(core == 0, low, high)
        out[:, lanes(k, 1)] = jnp.where(core == 0, high, low)


def images_of(img, k):
    return jnp.concatenate([img[h, k * SH : (k + 1) * SH] for h in range(2)], axis=0)


def partners_of(meta_out, k):
    parts = [meta_out[0:1, lanes(k, h)] * 128.0 + meta_out[1:2, lanes(k, h)] for h in range(2)]
    return jnp.concatenate(parts, axis=1)


STEP = 32


def activate(logit, partner, bases, store):
    rows, width = logit.shape
    iota = lax.broadcasted_iota(jnp.int32, (STEP, width), 0).astype(F32)
    positive = jnp.zeros((8, width), F32)
    logs = jnp.zeros((8, width), F32)
    product = None
    count = 0
    for start in range(0, rows, STEP):
        chunk, inner = divmod(start, SH)
        value = logit[start : start + STEP, :] * (SCALE * LOG2E) + (SHIFT * LOG2E)
        mask = (partner - (bases[chunk] + inner).astype(F32)) == iota
        value = jnp.where(mask, -value, value)
        small = jnp.exp2(-jnp.abs(value))
        one = 1.0 + small
        up = jnp.maximum(value, 0.0)
        positive = positive + ((up[0:8] + up[8:16]) + (up[16:24] + up[24:32]))
        term = (one[0:8] * one[8:16]) * (one[16:24] * one[24:32])
        product = term if product is None else product * term
        count += 4
        if count == 56 or start + STEP == rows:
            logs = logs + jnp.log(product)
            product, count = None, 0
        if store is not None:
            sig = jnp.where(value >= 0, 1.0, small) / one
            store(start, jnp.where(mask, -sig, sig).astype(BF16))
    return positive * LN2 + logs


def first_kernel(learner, *refs):
    refs = list(refs)
    gs, ds = refs[:7], refs[7:14]
    refs = refs[14:]
    core = core_index()
    if learner:
        g_out, excess, meta, img, txt, logit0, logit1, g_own, meta_own, sems, g_sems = refs
    else:
        meta, excess, img, txt, logit0, logit1, sems = refs
    ks = range(7)
    waits = fetch(core, gs, ds, img, txt, sems, ks)
    meta_waits = fetch_meta(core, gs, ds, meta_own, sems, ks) if learner else []
    for k in ks:
        waits["t", k].wait()
    waits["i", 0, 0].wait()
    waits["i", 0, 1].wait()
    bases = [text_base(k, core) for k in ks]
    logits = (logit0, logit1)
    excess[...] = jnp.zeros((8, NI), F32)
    if learner:
        meta[...] = jnp.zeros((8, NI), F32)

    def multiply(k):
        logits[k % 2][...] = lax.dot_general(
            txt[0 : 7 * SH], images_of(img, k), (((1,), (1,)), ((), ())), preferred_element_type=F32
        )

    copies = []

    def rest(k):
        store = None
        if learner:

            def store(start, value):
                for h in range(2):
                    g_own[start : start + STEP, lanes(k, h)] = value[:, h * SH : (h + 1) * SH]

        total = activate(logits[k % 2], partners_of(meta, k), bases, store)
        for h in range(2):
            excess[:, lanes(k, h)] = total[:, h * SH : (h + 1) * SH]
            if learner:
                at = (slice(0, 7 * SH), lanes(k, h))
                copy = pltpu.make_async_copy(g_own.at[at], g_out.at[at], g_sems.at[k, h])
                copy.start()
                copies.append(copy)

    for wait in meta_waits:
        wait.wait()
    if learner:
        spread_meta(core, meta_own, meta, ks)
    for k in range(1, 7):
        waits["i", k, 0].wait()
        waits["i", k, 1].wait()
    multiply(0)
    for k in range(1, 7):
        multiply(k)
        rest(k - 1)
    rest(6)
    for copy in copies:
        copy.wait()


def last_kernel(learner, *refs):
    refs = list(refs)
    gs, ds = refs[:8], refs[8:16]
    refs = refs[16:]
    core = core_index()
    if learner:
        before, _, g_out, excess, meta, img_out, txt_out = refs[:7]
        img, txt, logit0, logit1, g_own, meta_own, sems, g_sems = refs[7:]
    else:
        before, meta, learned, score, img, txt, logit0, logit1, sems = refs
    ks = (7, 0, 1, 2, 3, 4, 5, 6)
    waits = fetch(core, gs, ds, img, txt, sems, ks)
    meta_waits = fetch_meta(core, gs, ds, meta_own, sems, ks) if learner else []
    for k in ks:
        waits["t", k].wait()
    waits["i", 7, 0].wait()
    waits["i", 7, 1].wait()
    bases = [text_base(k, core) for k in range(8)]
    for wait in meta_waits:
        wait.wait()
    if learner:
        spread_meta(core, meta_own, meta, ks)
    logit0[...] = lax.dot_general(
        txt[0 : 7 * SH], images_of(img, 7), (((1,), (1,)), ((), ())), preferred_element_type=F32
    )
    for k in range(7):
        waits["i", k, 0].wait()
        waits["i", k, 1].wait()
    copies = []
    if learner:
        copies.append(pltpu.make_async_copy(img, img_out, g_sems.at[0]))
        copies.append(pltpu.make_async_copy(txt, txt_out, g_sems.at[1]))
        for copy in copies:
            copy.start()
    for h in range(2):
        logit1[:, h * NT : (h + 1) * NT] = lax.dot_general(
            txt[7 * SH :], img[h], (((1,), (1,)), ((), ())), preferred_element_type=F32
        )

    def store7(start, value):
        for h in range(2):
            g_own[start : start + STEP, lanes(7, h)] = value[:, h * SH : (h + 1) * SH]

    added = activate(logit0, partners_of(meta, 7), bases, store7 if learner else None)
    totals = {}
    for h in range(2):
        totals[7, h] = added[:, h * SH : (h + 1) * SH]
        if learner:
            at = (slice(0, 7 * SH), lanes(7, h))
            copy = pltpu.make_async_copy(g_own.at[at], g_out.at[at], g_sems.at[2 + h])
            copy.start()
            copies.append(copy)
    for k in range(8):
        for h in range(2):
            at = lanes(k, h)
            partner = meta[0:1, at] * 128.0 + meta[1:2, at]

            def store(start, value, at=at):
                g_own[7 * SH + start : 7 * SH + start + STEP, at] = value

            total = activate(logit1.at[:, at], partner, bases[7:], store if learner else None)
            total = total + (totals[7, h] if k == 7 else before[:, at])
            if learner:
                excess[:, at] = total
            else:
                totals[k, h] = learned[:, at] - total
    if learner:
        at = slice(7 * SH, NT)
        copy = pltpu.make_async_copy(g_own.at[at], g_out.at[at], g_sems.at[4])
        copy.start()
        copies.append(copy)
        for copy in copies:
            copy.wait()
    else:
        result = jnp.zeros((8, 2 * SPANS), F32)
        span = lax.broadcasted_iota(jnp.int32, (2 * SPANS, NT), 0).astype(F32)
        for h in range(2):
            table = (meta[2:3, h * NT : (h + 1) * NT] == span).astype(F32)
            excess = jnp.concatenate([totals[k, h] for k in range(8)], axis=1)
            result = result + lax.dot_general(
                excess,
                table,
                (((1,), (1,)), ((), ())),
                precision=lax.Precision.HIGHEST,
                preferred_element_type=F32,
            )
        score[...] = jnp.broadcast_to(jnp.sum(result, axis=0, keepdims=True), score.shape)


ANY = pl.BlockSpec(memory_space=pl.ANY)
VM = pl.BlockSpec(memory_space=pltpu.VMEM)


def scratch(first, learner):
    shapes = [
        pltpu.VMEM((2, NT, D), BF16),
        pltpu.VMEM((NT, D), BF16),
        pltpu.VMEM((7 * SH, CH), F32),
        pltpu.VMEM((7 * SH, CH) if first else (SH, NI), F32),
    ]
    if learner:
        shapes += [pltpu.VMEM((NT, NI), BF16), pltpu.VMEM((8, META, CH), BF16)]
    shapes.append(pltpu.SemaphoreType.DMA((8, 4)))
    if learner:
        shapes.append(pltpu.SemaphoreType.DMA((8, 2) if first else (5,)))
    return shapes


def cost(texts, images, learner):
    return pl.CostEstimate(
        flops=2 * texts * images * D,
        bytes_accessed=2 * (texts + images) * D,
        transcendentals=texts * images * (2 if learner else 1),
    )


def shape(rows, columns, kind):
    return jax.ShapeDtypeStruct((rows, columns), kind)


def learner_first(gs, ds):
    return pl.pallas_call(
        functools.partial(first_kernel, True),
        out_shape=(shape(NT, NI, BF16), shape(8, NI, F32), shape(8, NI, F32)),
        in_specs=[ANY] * 14,
        out_specs=(ANY, VM, VM),
        scratch_shapes=scratch(True, True),
        compiler_params=params(32),
        cost_estimate=cost(7 * SH, 7 * CH, True),
    )(*gs, *ds)


def learner_last(gs, ds, excess, g):
    return pl.pallas_call(
        functools.partial(last_kernel, True),
        out_shape=(
            shape(NT, NI, BF16),
            shape(8, NI, F32),
            shape(8, NI, F32),
            jax.ShapeDtypeStruct((2, NT, D), BF16),
            shape(NT, D, BF16),
        ),
        in_specs=[ANY] * 16 + [VM, ANY],
        out_specs=(ANY, VM, VM, ANY, ANY),
        scratch_shapes=scratch(False, True),
        input_output_aliases={17: 0},
        compiler_params=params(32),
        cost_estimate=cost(SH, NI + 7 * CH, True),
    )(*gs, *ds, excess, g)


def refer_first(gs, ds, meta):
    return pl.pallas_call(
        functools.partial(first_kernel, False),
        out_shape=shape(8, NI, F32),
        in_specs=[ANY] * 14 + [VM],
        out_specs=VM,
        scratch_shapes=scratch(True, False),
        compiler_params=params(32),
        cost_estimate=cost(7 * SH, 7 * CH, False),
    )(*gs, *ds, meta)


def refer_last(gs, ds, before, meta, learned):
    return pl.pallas_call(
        functools.partial(last_kernel, False),
        out_shape=shape(8, 2 * SPANS, F32),
        in_specs=[ANY] * 16 + [VM, VM, VM],
        out_specs=VM,
        scratch_shapes=scratch(False, False),
        compiler_params=params(32),
        cost_estimate=cost(SH, NI + 7 * CH, False),
    )(*gs, *ds, before, meta, learned)


def image_kernel(g, txt, out):
    out[...] = lax.dot_general(
        g[...], txt[...], (((0,), (0,)), ((), ())), preferred_element_type=F32
    ).astype(BF16)


def image_part(g, txt, half):
    return pl.pallas_call(
        image_kernel,
        grid=(4,),
        out_shape=shape(NT, D, BF16),
        in_specs=[
            pl.BlockSpec((NT, CH), lambda i: (0, 4 * half + i)),
            pl.BlockSpec((NT, D), lambda i: (0, 0)),
        ],
        out_specs=pl.BlockSpec((CH, D), lambda i: (i, 0)),
        compiler_params=params(24),
        cost_estimate=pl.CostEstimate(
            flops=2 * NT * NT * D, bytes_accessed=6 << 20, transcendentals=0
        ),
    )(g, txt)


TK = 512


def text_kernel(score, meta, g, img, out, total):
    step = pl.program_id(0)
    weight = jax.nn.sigmoid(SHARP * score[...] / GROUP)
    span = lax.broadcasted_iota(jnp.int32, (2 * SPANS, TK), 0).astype(F32)
    table = (meta[2:3, :] == span).astype(F32)
    rows = jnp.dot(weight, table, precision=lax.Precision.HIGHEST, preferred_element_type=F32)
    rows = rows[0:1] * jnp.where(meta[3:4, :] == 1.0, SCALE * SYNTH, SCALE)
    weighted = (g[...].astype(F32) * rows).astype(BF16)
    part = jnp.dot(weighted, img[...], preferred_element_type=F32)

    @pl.when(step == 0)
    def _():
        total[...] = part

    @pl.when(jnp.logical_and(step > 0, step < NI // TK - 1))
    def _():
        total[...] += part

    @pl.when(step == NI // TK - 1)
    def _():
        out[...] = (total[...] + part).astype(BF16)


def text_part(score, meta, g, img, half):
    rows = NT // 2
    return pl.pallas_call(
        text_kernel,
        grid=(NI // TK,),
        out_shape=shape(rows, D, BF16),
        in_specs=[
            pl.BlockSpec((8, 2 * SPANS), lambda i: (0, 0)),
            pl.BlockSpec((8, TK), lambda i: (0, i)),
            pl.BlockSpec((rows, TK), lambda i: (half, i)),
            pl.BlockSpec((TK, D), lambda i: (i, 0)),
        ],
        out_specs=pl.BlockSpec((rows, D), lambda i: (0, 0)),
        scratch_shapes=[pltpu.VMEM((rows, D), F32)],
        compiler_params=params(24),
        cost_estimate=pl.CostEstimate(
            flops=2 * rows * NI * D, bytes_accessed=8 << 20, transcendentals=0
        ),
    )(score, meta, g, img)


def add(*terms):
    return sum(t.astype(F32) for t in terms)


def cube_scatter(chunks, kind):
    own, X, Y, Z, XY, YZ, ZX, XYZ = chunks
    to_yz = swap(XYZ, "x", kind)
    to_x = [swap(XY, "y", kind), swap(ZX, "z", kind)]
    to_z = swap(add(YZ, to_yz).astype(BF16), "y", kind)
    from_x = swap(add(X, *to_x).astype(BF16), "x", kind)
    from_y = swap(Y, "y", kind)
    from_z = swap(add(Z, to_z).astype(BF16), "z", kind)
    return add(own, from_x, from_y, from_z)


def all_sum(score):
    score = score + swap(score, "c")
    for axis in "xyz":
        for kind in (0, 1):
            score = score + swap(score, axis, kind)
    return score


def parts_of(array, count):
    return [array[i * SH : (i + 1) * SH] for i in range(count)]


def shards(img_learner, txt_learner, img_ref, txt_ref, partner, synthetic, span_ids):
    meta = jnp.stack([partner, synthetic, span_ids])
    own_learn = payload(img_learner, txt_learner, meta)
    own_refer = payload(img_ref, txt_ref)
    g_learn = cube_gather(own_learn, "x")
    g_refer = cube_gather(own_refer, "y")
    d_learn = [swap(v, "c") for v in g_learn]
    d_refer = [swap(v, "c") for v in g_refer]

    grad, excess, meta7 = learner_first(g_learn[:7], d_learn[:7])
    before = refer_first(g_refer[:7], d_refer[:7], meta7)
    grad, excess, meta8, img, txt = learner_last(g_learn, d_learn, excess, grad)
    partial = refer_last(g_refer, d_refer, before, meta8, excess)
    score = all_sum(partial)

    img_send = image_part(grad, txt, 1)
    img_keep = image_part(grad, txt, 0)
    img_sum = add(img_keep, swap(img_send, "c")).astype(BF16)
    img_total = cube_scatter(parts_of(img_sum, 8), 0)

    img = img.reshape(NI, D)
    far = text_part(score, meta8, grad, img, 1)
    near = text_part(score, meta8, grad, img, 0)
    txt_grad = cube_scatter(parts_of(near, 4) + parts_of(far, 4), 1).astype(BF16)

    span_weight = jax.nn.sigmoid(SHARP * score[0, :SPANS] / GROUP)
    table = span_ids[:, None] == jnp.arange(SPANS, dtype=jnp.int32)[None, :]
    row_weight = jnp.sum(jnp.where(table, span_weight[None, :], 0.0), axis=1, keepdims=True)
    row_weight = row_weight * jnp.where(synthetic == 1, SCALE * SYNTH, SCALE)[:, None]
    img_grad = (img_total * row_weight).astype(BF16)
    return img_grad, txt_grad, span_weight


def solution(mesh):
    placed = (
        P(("row", "col"), None),
        P(("col", "row"), None),
        P(("row", "col"), None),
        P(("col", "row"), None),
        P(("row", "col")),
        P(("row", "col")),
        P(("row", "col")),
    )
    return jax.shard_map(
        shards,
        mesh=mesh,
        in_specs=placed,
        out_specs=(P(("row", "col"), None), P(("col", "row"), None), P()),
        check_vma=False,
    )
```

```python
import functools

import jax
import jax.numpy as jnp
from jax import lax
from jax.experimental import pallas as pl
from jax.experimental.pallas import tpu as pltpu
from jax.sharding import PartitionSpec as P

SPANS = 64
D = 1152
SH = 128
CH = 2 * SH
NT = 8 * SH
NI = 8 * CH
META = 16
REFER = CH + META
ROWS = REFER + CH
GROUP = 256.0
SCALE = 10.0
SHIFT = -5.0
SHARP = 5.0
SYNTH = 0.5
LN2 = 0.6931471805599453
LOG2E = 1.4426950408889634
AXES = ("row", "col")
F32 = jnp.float32
BF16 = jnp.bfloat16
MIB = 1 << 20

FLIPS = ("", "x", "y", "z", "xy", "yz", "zx", "xyz")


def place(index):
    row, col = divmod(index, 16)
    return dict(z=row // 2, y=2 * (row % 2) + col // 8, x=(col // 2) % 4, c=col % 2)


def device(z, y, x, c):
    return (2 * z + y // 2) * 16 + 8 * (y % 2) + 2 * x + c


def pairs(axis, kind):
    out = []
    for index in range(128):
        at = place(index)
        if axis == "c":
            at["c"] ^= 1
        else:
            k = at["c"] if kind == "mixed" else kind
            at[axis] = at[axis] ^ 1 if k == 0 else 3 - at[axis]
        out.append((index, device(**at)))
    return out


SWAP = {(a, k): pairs(a, k) for a in "xyz" for k in (0, 1, "mixed")}
SWAP["c"] = pairs("c", 0)


def swap(value, axis, kind=0):
    return lax.ppermute(value, AXES, SWAP["c"] if axis == "c" else SWAP[axis, kind])


HBM = pl.BlockSpec(memory_space=pltpu.HBM)
VM = pl.BlockSpec(memory_space=pltpu.VMEM)


def params(mib):
    return pltpu.CompilerParams(vmem_limit_bytes=mib * MIB)


def core_index():
    return lax.rem(lax.axis_index("col"), 2)


def payload_kernel(img_l, txt_l, img_r, txt_r, oimg_l, otxt_l, oimg_r, otxt_r, meta, ometa, out, sems):
    core = core_index()
    copies = []
    for side, place, mine, other in (
        (0, 0, (img_l, txt_l), (oimg_l, otxt_l)),
        (1, REFER, (img_r, txt_r), (oimg_r, otxt_r)),
    ):

        @pl.when(core == 0)
        def _():
            pltpu.make_async_copy(mine[0], out.at[place : place + SH], sems.at[side]).start()
            out[place + SH : place + CH] = other[0][...]

        @pl.when(core == 1)
        def _():
            pltpu.make_async_copy(mine[1], out.at[place + SH : place + CH], sems.at[side]).start()
            out[place : place + SH] = other[1][...]

        copies.append(pltpu.make_async_copy(mine[0], out.at[place : place + SH], sems.at[side]))
    out[CH:REFER] = jnp.zeros((META, D), BF16)
    row = lax.broadcasted_iota(jnp.int32, (META, SH), 0)
    for side, ref in enumerate((meta, ometa)):
        partner, synth, span = (ref[i : i + 1, :] for i in range(3))
        block = jnp.where(row == 0, lax.shift_right_logical(partner, 7), 0)
        block = jnp.where(row == 1, partner & 127, block)
        block = jnp.where(row == 2, span, block)
        block = jnp.where(row == 3, synth, block)
        out[CH:REFER, side * SH : (side + 1) * SH] = block.astype(F32).astype(BF16)
    for copy in copies:
        copy.wait()


def payload(mine, others, meta, other_meta):
    return pl.pallas_call(
        payload_kernel,
        out_shape=jax.ShapeDtypeStruct((ROWS, D), BF16),
        in_specs=[HBM] * 4 + [VM] * 6,
        out_specs=VM,
        scratch_shapes=[pltpu.SemaphoreType.DMA((2,))],
        compiler_params=params(8),
        cost_estimate=pl.CostEstimate(flops=0, bytes_accessed=1 << 21, transcendentals=0),
    )(*mine, *others, meta, other_meta)


def after(value, *others):
    return lax.optimization_barrier((value, others))[0]


def cube_near(own):
    return [own] + [swap(own, axis, "mixed") for axis in "xyz"]


def cube_edges(X, Y, Z):
    return [swap(Y, "x", "mixed"), swap(Z, "y", "mixed"), swap(X, "z", "mixed")]


def halves_kernel(yz, zx, learn, refer):
    learn[...] = yz[:REFER]
    refer[...] = zx[REFER:]


def cube_corner(XY, YZ, ZX):
    estimate = pl.CostEstimate(flops=0, bytes_accessed=4 << 20, transcendentals=0)
    outs = [(REFER, D, BF16), (CH, D, BF16)]
    learn, refer = call(halves_kernel, [YZ, ZX], outs, [], estimate)
    return [swap(learn, "x", "mixed"), swap(refer, "y", "mixed")]


def text_base(k, core):
    row, col = lax.axis_index("row"), lax.axis_index("col")
    z, yh = row // 2, lax.rem(row, 2)
    yl, x = col // 8, lax.rem(col // 2, 4)
    y = 2 * yh + yl
    x = 3 - x if "x" in FLIPS[k] else x
    y = 3 - y if "y" in FLIPS[k] else y
    z = 3 - z if "z" in FLIPS[k] else z
    col = 8 * lax.rem(y, 2) + 2 * x + core
    row = 2 * z + y // 2
    return (col * 8 + row) * SH


HALF = slice(0, SH), slice(SH, CH)


def pick(core, g, d, base, rows, half):
    mine, other = HALF[half], HALF[1 - half]
    at = slice(base + mine.start, base + mine.stop), slice(base + other.start, base + other.stop)
    return jnp.where(core == 0, g[at[0], :], d[at[1], :]) if rows == "images" else jnp.where(
        core == 0, d[at[0], :], g[at[1], :]
    )


def lanes(k, h):
    return slice(h * NT + k * SH, h * NT + (k + 1) * SH)


def product(left, right):
    return lax.dot_general(left, right, (((1,), (1,)), ((), ())), preferred_element_type=F32)


STEP = 32


def fold(value):
    return (value[0:8] + value[8:16]) + (value[16:24] + value[24:32])


def fold_product(value):
    return (value[0:8] * value[8:16]) * (value[16:24] * value[24:32])


def inverse(value):
    guess = pltpu.reciprocal(value, approx=True)
    return guess * (2.0 - value * guess)


def activate(learn, refer, partner, bases, store):
    rows, width = learn.shape
    iota = lax.broadcasted_iota(jnp.int32, (STEP, width), 0).astype(F32)
    positive = jnp.zeros((8, width), F32)
    logs = jnp.zeros((8, width), F32)
    factors = None
    count = 0
    for start in range(0, rows, STEP):
        chunk, inner = divmod(start, SH)
        mask = (partner - (bases[chunk] + inner).astype(F32)) == iota

        def part(ref):
            value = ref[start : start + STEP, :] * (SCALE * LOG2E) + (SHIFT * LOG2E)
            value = jnp.where(mask, -value, value)
            small = jnp.exp2(-jnp.abs(value))
            return value, small, 1.0 + small

        value, small, one = part(learn)
        value_r, _, one_r = part(refer)
        positive = positive + fold(jnp.maximum(value, 0.0) - jnp.maximum(value_r, 0.0))
        terms = fold_product(one), fold_product(one_r)
        factors = terms if factors is None else (factors[0] * terms[0], factors[1] * terms[1])
        count += 4
        if count == 64 or start + STEP == rows:
            logs = logs + (jnp.log(factors[0]) - jnp.log(factors[1]))
            factors, count = None, 0
        sig = jnp.where(value >= 0, 1.0, small) * inverse(one)
        store(start, jnp.where(mask, -sig, sig).astype(BF16))
    return positive * LN2 + logs


STAGES = (
    ((0, 1, 2, 3), [(0, 4, k) for k in range(4)]),
    ((4, 5, 6), [(0, 7, k) for k in (4, 5, 6)]),
    ((), [(4, 7, k) for k in range(4)]),
    ((7,), [(0, 8, 7)] + [(7, 8, k) for k in range(7)]),
)


def stage_kernel(stage, *refs):
    new, blocks = STAGES[stage]
    refs = list(refs)
    last = stage == len(STAGES) - 1
    if last:
        gs, ds, refs = [(refs[0], refs[1])], [(refs[2], refs[3])], refs[4:]
    else:
        count = len(new)
        gs, ds, refs = [(v, v) for v in refs[:count]], [(v, v) for v in refs[count : 2 * count]], refs[2 * count :]
    if stage > 0:
        refs = refs[len(STATE) :]
    grad, excess, meta, img_l, txt_l, img_r, txt_r = refs[: len(STATE)]
    refs = refs[len(STATE) :]
    if last:
        score, refs = refs[0], refs[1:]
    logits = refs
    core = core_index()
    models = ((0, img_l, txt_l), (0 if last else REFER, img_r, txt_r))
    for k, g, d in zip(new, gs, ds):
        for model, (base, img, txt) in enumerate(models):
            txt[k * SH : (k + 1) * SH] = pick(core, g[model], d[model], base, "texts", 0)
            for h in range(2):
                img[lanes(k, h)] = pick(core, g[model], d[model], base, "images", h)
        for h in range(2):
            block = jnp.where(core == 0, g[0][CH:REFER, HALF[h]], d[0][CH:REFER, HALF[1 - h]])
            meta[:, lanes(k, h)] = block.astype(F32)[0:8]
    bases = [text_base(k, core) for k in range(8)]

    def multiply(index):
        first, end, k = blocks[index]
        for model, (_, img, txt) in enumerate(models):
            images = jnp.concatenate([img[lanes(k, h)] for h in range(2)], axis=0)
            logits[2 * (index % 2) + model][0 : (end - first) * SH] = product(txt[first * SH : end * SH], images)

    def rest(index):
        first, end, k = blocks[index]

        def store(start, value):
            row = first * SH + start
            for h in range(2):
                grad[row : row + STEP, lanes(k, h)] = value[:, HALF[h]]

        both = [meta[0:1, lanes(k, h)] * 128.0 + meta[1:2, lanes(k, h)] for h in range(2)]
        rows = slice(0, (end - first) * SH)
        learn, refer = (logits[2 * (index % 2) + model].at[rows] for model in range(2))
        total = activate(learn, refer, jnp.concatenate(both, axis=1), bases[first:end], store)
        for h in range(2):
            if first == 0:
                excess[:, lanes(k, h)] = total[:, HALF[h]]
            else:
                excess[:, lanes(k, h)] += total[:, HALF[h]]

    multiply(0)
    for index in range(len(blocks)):
        if index + 1 < len(blocks):
            multiply(index + 1)
        rest(index)
    if last:
        span = lax.broadcasted_iota(jnp.int32, (SPANS, SH), 0).astype(F32)
        table = jnp.zeros((SPANS, SH), F32)
        for start in range(0, NI, SH):
            at = slice(start, start + SH)
            part = jnp.sum(excess[:, at], axis=0, keepdims=True)
            table = table + jnp.where(meta[2:3, at] == span, part, 0.0)
        table = jnp.concatenate([table, jnp.zeros((SH - SPANS, SH), F32)], axis=0)
        result = jnp.sum(jnp.transpose(table), axis=0, keepdims=True)
        score[...] = jnp.broadcast_to(result, score.shape)


def shape(rows, columns, kind):
    return jax.ShapeDtypeStruct((rows, columns), kind)


def call(body, args, outs, scratch, estimate, aliases={}, mib=20):
    return pl.pallas_call(
        body,
        out_shape=tuple(shape(*out) for out in outs),
        in_specs=[VM] * len(args),
        out_specs=(VM,) * len(outs),
        scratch_shapes=[pltpu.VMEM((rows, columns), kind) for rows, columns, kind in scratch],
        input_output_aliases=aliases,
        compiler_params=params(mib),
        cost_estimate=estimate,
    )(*args)


STATE = [
    (NT, NI, BF16),
    (8, NI, F32),
    (8, NI, F32),
    (NI, D, BF16),
    (NT, D, BF16),
    (NI, D, BF16),
    (NT, D, BF16),
]


def run_stage(stage, chunks, state):
    new, blocks = STAGES[stage]
    texts = max(end - first for first, end, _ in blocks) * SH
    pairs_done = sum((end - first) * SH * CH for first, end, _ in blocks)
    estimate = pl.CostEstimate(
        flops=4 * pairs_done * D, bytes_accessed=8 << 20, transcendentals=3 * pairs_done
    )
    last = stage == len(STAGES) - 1
    outs = STATE + ([(8, SH, F32)] if last else [])
    aliases = {len(chunks) + i: i for i in range(len(STATE))} if stage else {}
    scratch = [(texts, CH, F32)] * 4
    args = [*chunks, *(state if stage else [])]
    return call(functools.partial(stage_kernel, stage), args, outs, scratch, estimate, aliases)


def image_kernel(half, grad, txt, out):
    out[...] = lax.dot_general(
        grad[:, half * NT : (half + 1) * NT],
        txt[...],
        (((0,), (0,)), ((), ())),
        preferred_element_type=F32,
    ).astype(BF16)


def image_part(grad, txt, half):
    body = functools.partial(image_kernel, half)
    estimate = pl.CostEstimate(flops=2 * NT * NT * D, bytes_accessed=6 << 20, transcendentals=0)
    return call(body, [grad, txt], [(NT, D, BF16)], [], estimate)[0]


def text_kernel(far, score, meta, grad, img, part, other_part, all_texts, *rest):
    *outs, weighted = rest
    weight = jax.nn.sigmoid(SHARP * score[0:1, :] / GROUP)
    column = jnp.transpose(jnp.broadcast_to(weight, (SH, SH)))[0:SPANS]
    span = lax.broadcasted_iota(jnp.int32, (SPANS, SH), 0).astype(F32)
    rows = slice(far * 4 * SH, (far + 1) * 4 * SH)
    for start in range(0, NI, SH):
        at = slice(start, start + SH)
        chosen = jnp.where(meta[2:3, at] == span, column, 0.0)
        factor = jnp.sum(chosen, axis=0, keepdims=True)
        factor = factor * jnp.where(meta[3:4, at] == 1.0, SCALE * SYNTH, SCALE)
        weighted[:, at] = (grad[rows, at].astype(F32) * factor).astype(BF16)
    total = jnp.dot(weighted[...], img[...], preferred_element_type=F32)
    for k, out in enumerate(outs):
        at = slice(rows.start + k * SH, rows.start + (k + 1) * SH)
        images = part[at].astype(F32) + other_part[at].astype(F32)
        texts = total[k * SH : (k + 1) * SH]
        all_texts[k * SH : (k + 1) * SH] = texts.astype(BF16)
        out[...] = jnp.where(core_index() == 0, images, texts).astype(BF16)


def text_part(score, meta, grad, img, part, other_part, far):
    rows = 4 * SH
    body = functools.partial(text_kernel, far)
    estimate = pl.CostEstimate(flops=2 * rows * NI * D, bytes_accessed=8 << 20, transcendentals=0)
    outs = [(rows, D, BF16)] + [(SH, D, BF16)] * 4
    args = [score, meta, grad, img, part, other_part]
    texts, *chunks = call(body, args, outs, [(rows, NI, BF16)], estimate)
    return texts, chunks


def second_kernel(far, part, other_part, texts, *outs):
    for k, out in enumerate(outs):
        at = slice((far * 4 + k) * SH, (far * 4 + k + 1) * SH)
        images = part[at].astype(F32) + other_part[at].astype(F32)
        chunk = texts[k * SH : (k + 1) * SH].astype(F32)
        out[...] = jnp.where(core_index() == 0, images, chunk).astype(BF16)


def second_part(part, other_part, texts, far):
    body = functools.partial(second_kernel, far)
    estimate = pl.CostEstimate(flops=0, bytes_accessed=4 << 20, transcendentals=0)
    return call(body, [part, other_part, texts], [(SH, D, BF16)] * 4, [], estimate)


def add(*terms):
    return sum(t.astype(F32) for t in terms)


def cube_first(chunks, kind):
    XY, YZ, ZX, XYZ = chunks
    return swap(XYZ, "x", kind), swap(XY, "y", kind), swap(ZX, "z", kind)


def cube_rest(near, yz, first, kind):
    own, X, Y, Z = near
    to_yz, *to_x = first
    to_z = swap(add(yz, to_yz).astype(BF16), "y", kind)
    from_x = swap(add(X, *to_x).astype(BF16), "x", kind)
    from_y = swap(Y, "y", kind)
    from_z = swap(add(Z, to_z).astype(BF16), "z", kind)
    return add(own, from_x, from_y, from_z)


def shards(img_learner, txt_learner, img_ref, txt_ref, partner, synthetic, span_ids):
    mine = [img_learner, txt_learner, img_ref, txt_ref]
    meta = jnp.stack([partner, synthetic, span_ids])
    others = [swap(v, "c") for v in mine]
    own = payload(mine, others, meta, swap(meta, "c"))
    near = cube_near(own)
    state = run_stage(0, near + [swap(v, "c") for v in near], None)
    edges = cube_edges(*near[1:])
    corner = cube_corner(*edges)
    state = run_stage(1, edges + [swap(v, "c") for v in edges], state)
    other_corner = [swap(v, "c") for v in after(corner, state[1])]
    state = run_stage(2, [], state)
    *state, partial = run_stage(3, corner + other_corner, state)
    grad, _, meta, img, txt, _, _ = state

    score = partial + swap(partial, "c")
    score = score + swap(score, "x", 0)
    part0 = image_part(grad, after(txt, score), 0)
    score = after(score + swap(score, "x", 1), part0)
    other0 = swap(after(part0, score), "c")
    part1 = image_part(grad, after(txt, score), 1)
    score = after(score + swap(score, "y", 0), part1)
    score = score + swap(score, "y", 1)
    other1 = swap(after(part1, score), "c")
    score = score + swap(score, "z", 0)
    score = score + swap(score, "z", 1)

    texts, far_b = text_part(score, meta, grad, img, part1, other0, 1)
    first_b = cube_first(far_b, "mixed")
    far_a = second_part(part0, other1, swap(texts, "c"), 1)
    first_a = cube_first(far_a, "mixed")
    texts, near_b = text_part(score, meta, grad, after(img, first_a[0]), part1, other0, 0)
    sum_b = cube_rest(near_b, far_b[1], first_b, "mixed").astype(BF16)
    near_a = second_part(part0, other1, swap(texts, "c"), 0)
    sum_a = cube_rest(near_a, far_a[1], first_a, "mixed").astype(BF16)
    core = core_index()
    moved = swap(jnp.where(core == 0, sum_b, sum_a), "c")
    img_total = jnp.where(core == 0, sum_a, moved).astype(F32)
    txt_grad = jnp.where(core == 0, moved, sum_b)

    span_weight = jax.nn.sigmoid(SHARP * score[0, :SPANS] / GROUP)
    table = span_ids[:, None] == jnp.arange(SPANS, dtype=jnp.int32)[None, :]
    row_weight = jnp.sum(jnp.where(table, span_weight[None, :], 0.0), axis=1, keepdims=True)
    row_weight = row_weight * jnp.where(synthetic == 1, SCALE * SYNTH, SCALE)[:, None]
    img_grad = (img_total * row_weight).astype(BF16)
    return img_grad, txt_grad, span_weight


def solution(mesh):
    placed = (
        P(("row", "col"), None),
        P(("col", "row"), None),
        P(("row", "col"), None),
        P(("col", "row"), None),
        P(("row", "col")),
        P(("row", "col")),
        P(("row", "col")),
    )
    return jax.shard_map(
        shards,
        mesh=mesh,
        in_specs=placed,
        out_specs=(P(("row", "col"), None), P(("col", "row"), None), P()),
        check_vma=False,
    )
```

```python
import functools

import jax
import jax.numpy as jnp
from jax import lax
from jax.experimental import pallas as pl
from jax.experimental.pallas import tpu as pltpu
from jax.sharding import PartitionSpec as P

SPANS = 64
D = 1152
SH = 128
CH = 2 * SH
NT = 8 * SH
NI = 8 * CH
META = 16
REFER = CH + META
ROWS = REFER + CH
GROUP = 256.0
SCALE = 10.0
SHIFT = -5.0
SHARP = 5.0
SYNTH = 0.5
LN2 = 0.6931471805599453
LOG2E = 1.4426950408889634
AXES = ("row", "col")
F32 = jnp.float32
BF16 = jnp.bfloat16
MIB = 1 << 20

FLIPS = ("", "x", "y", "z", "xy", "yz", "zx", "xyz")


def place(index):
    row, col = divmod(index, 16)
    return dict(z=row // 2, y=2 * (row % 2) + col // 8, x=(col // 2) % 4, c=col % 2)


def device(z, y, x, c):
    return (2 * z + y // 2) * 16 + 8 * (y % 2) + 2 * x + c


def pairs(axes, kind):
    out = []
    for index in range(128):
        at = place(index)
        k = at["c"] if kind == "mixed" else kind
        for axis in axes:
            if axis == "c":
                at["c"] ^= 1
            else:
                at[axis] = at[axis] ^ 1 if k == 0 else 3 - at[axis]
        out.append((index, device(**at)))
    return out


def swap(value, axes, kind=0):
    return lax.ppermute(value, AXES, pairs(axes, kind))


VM = pl.BlockSpec(memory_space=pltpu.VMEM)


def params(mib):
    return pltpu.CompilerParams(vmem_limit_bytes=mib * MIB)


def core_index():
    return lax.rem(lax.axis_index("col"), 2)


def payload_kernel(mine_l, mine_r, oimg_l, otxt_l, oimg_r, otxt_r, meta, ometa, out):
    core = core_index()
    for place, mine, images, texts in ((0, mine_l, oimg_l, otxt_l), (REFER, mine_r, oimg_r, otxt_r)):
        out[place : place + SH] = jnp.where(core == 0, mine[...], texts[...])
        out[place + SH : place + CH] = jnp.where(core == 0, images[...], mine[...])
    out[CH:REFER] = jnp.zeros((META, D), BF16)
    row = lax.broadcasted_iota(jnp.int32, (META, SH), 0)
    for side, ref in enumerate((meta, ometa)):
        partner, synth, span = (ref[i : i + 1, :] for i in range(3))
        block = jnp.where(row == 0, lax.shift_right_logical(partner, 7), 0)
        block = jnp.where(row == 1, partner & 127, block)
        block = jnp.where(row == 2, span, block)
        block = jnp.where(row == 3, synth, block)
        out[CH:REFER, side * SH : (side + 1) * SH] = block.astype(F32).astype(BF16)


def payload(mine, others, meta, other_meta):
    estimate = pl.CostEstimate(flops=0, bytes_accessed=1 << 21, transcendentals=0)
    args = [*mine, *others, meta, other_meta]
    return call(payload_kernel, args, [(ROWS, D, BF16)], [], estimate, mib=8)[0]


def after(value, *others):
    return lax.optimization_barrier((value, others))[0]


def cube_near(own):
    return [own] + [swap(own, axis, "mixed") for axis in "xyz"]


def cube_edges(X, Y, Z):
    return [swap(Y, "x", "mixed"), swap(Z, "y", "mixed"), swap(X, "z", "mixed")]


def halves_kernel(yz, zx, learn, refer):
    learn[...] = yz[:REFER]
    refer[...] = zx[REFER:]


def cube_corner(XY, YZ, ZX):
    estimate = pl.CostEstimate(flops=0, bytes_accessed=4 << 20, transcendentals=0)
    outs = [(REFER, D, BF16), (CH, D, BF16)]
    learn, refer = call(halves_kernel, [YZ, ZX], outs, [], estimate)
    return [swap(learn, "x", "mixed"), swap(refer, "y", "mixed")]


def text_base(k, core):
    row, col = lax.axis_index("row"), lax.axis_index("col")
    z, yh = row // 2, lax.rem(row, 2)
    yl, x = col // 8, lax.rem(col // 2, 4)
    y = 2 * yh + yl
    x = 3 - x if "x" in FLIPS[k] else x
    y = 3 - y if "y" in FLIPS[k] else y
    z = 3 - z if "z" in FLIPS[k] else z
    col = 8 * lax.rem(y, 2) + 2 * x + core
    row = 2 * z + y // 2
    return (col * 8 + row) * SH


HALF = slice(0, SH), slice(SH, CH)


def pick(core, g, d, base, rows, half):
    mine, other = HALF[half], HALF[1 - half]
    at = slice(base + mine.start, base + mine.stop), slice(base + other.start, base + other.stop)
    return jnp.where(core == 0, g[at[0], :], d[at[1], :]) if rows == "images" else jnp.where(
        core == 0, d[at[0], :], g[at[1], :]
    )


def lanes(k, h):
    if isinstance(k, int):
        return slice(h * NT + k * SH, h * NT + (k + 1) * SH)
    return pl.ds(pl.multiple_of(h * NT + k * SH, SH), SH)


def product(left, right):
    return lax.dot_general(left, right, (((1,), (1,)), ((), ())), preferred_element_type=F32)


STEP = 32


def fold(value):
    return (value[0:8] + value[8:16]) + (value[16:24] + value[24:32])


def fold_product(value):
    return (value[0:8] * value[8:16]) * (value[16:24] * value[24:32])


def inverse(value):
    guess = pltpu.reciprocal(value, approx=True)
    return guess * (2.0 - value * guess)


def activate(learn, refer, partner, bases, store):
    rows, width = learn.shape
    iota = lax.broadcasted_iota(jnp.int32, (STEP, width), 0).astype(F32)
    positive = jnp.zeros((8, width), F32)
    logs = jnp.zeros((8, width), F32)
    factors = None
    count = 0
    for start in range(0, rows, STEP):
        chunk, inner = divmod(start, SH)
        mask = (partner - (bases[chunk] + inner).astype(F32)) == iota

        def part(ref):
            value = ref[start : start + STEP, :] * (SCALE * LOG2E) + (SHIFT * LOG2E)
            value = jnp.where(mask, -value, value)
            small = jnp.exp2(-jnp.abs(value))
            return value, small, 1.0 + small

        value, small, one = part(learn)
        value_r, _, one_r = part(refer)
        positive = positive + fold(jnp.maximum(value, 0.0) - jnp.maximum(value_r, 0.0))
        terms = fold_product(one), fold_product(one_r)
        factors = terms if factors is None else (factors[0] * terms[0], factors[1] * terms[1])
        count += 4
        if count == 64 or start + STEP == rows:
            logs = logs + (jnp.log(factors[0]) - jnp.log(factors[1]))
            factors, count = None, 0
        sig = jnp.where(value >= 0, 1.0, small) * inverse(one)
        store(start, jnp.where(mask, -sig, sig).astype(BF16))
    return positive * LN2 + logs


STAGES = (
    ((0, 1, 2, 3), [(0, 4, k) for k in range(4)]),
    ((4, 5, 6), [(0, 7, k) for k in (4, 5, 6)]),
    ((), [(4, 7, k) for k in range(4)]),
    ((7,), [(0, 8, 7)] + [(7, 8, k) for k in range(7)]),
)


LOOPS = (False, False, False, False)


def stage_kernel(stage, *refs):
    new, blocks = STAGES[stage]
    refs = list(refs)
    last = stage == len(STAGES) - 1
    if last:
        gs, ds, refs = [(refs[0], refs[1])], [(refs[2], refs[3])], refs[4:]
    else:
        count = len(new)
        gs, ds, refs = [(v, v) for v in refs[:count]], [(v, v) for v in refs[count : 2 * count]], refs[2 * count :]
    if stage > 0:
        refs = refs[len(STATE) :]
    grad, excess, meta, img_l, txt_l, img_r, txt_r = refs[: len(STATE)]
    refs = refs[len(STATE) :]
    if last:
        score, refs = refs[0], refs[1:]
    logits = refs
    core = core_index()
    models = ((0, img_l, txt_l), (0 if last else REFER, img_r, txt_r))
    for k, g, d in zip(new, gs, ds):
        for model, (base, img, txt) in enumerate(models):
            txt[k * SH : (k + 1) * SH] = pick(core, g[model], d[model], base, "texts", 0)
            for h in range(2):
                img[lanes(k, h)] = pick(core, g[model], d[model], base, "images", h)
        for h in range(2):
            block = jnp.where(core == 0, g[0][CH:REFER, HALF[h]], d[0][CH:REFER, HALF[1 - h]])
            meta[:, lanes(k, h)] = block.astype(F32)[0:8]
    bases = [text_base(k, core) for k in range(8)]

    def multiply(block, slot):
        first, end, k = block
        for model, (_, img, txt) in enumerate(models):
            images = jnp.concatenate([img[lanes(k, h), :] for h in range(2)], axis=0)
            logits[2 * slot + model][0 : (end - first) * SH] = product(txt[first * SH : end * SH], images)

    def rest(block, slot):
        first, end, k = block

        def store(start, value):
            row = first * SH + start
            for h in range(2):
                grad[row : row + STEP, lanes(k, h)] = value[:, HALF[h]]

        both = [meta[0:1, lanes(k, h)] * 128.0 + meta[1:2, lanes(k, h)] for h in range(2)]
        rows = slice(0, (end - first) * SH)
        learn, refer = (logits[2 * slot + model].at[rows] for model in range(2))
        total = activate(learn, refer, jnp.concatenate(both, axis=1), bases[first:end], store)
        for h in range(2):
            if first == 0:
                excess[:, lanes(k, h)] = total[:, HALF[h]]
            else:
                excess[:, lanes(k, h)] += total[:, HALF[h]]

    if LOOPS[stage]:
        first, end, _ = blocks[0]
        multiply(blocks[0], 0)

        @pl.loop(0, len(blocks) // 2)
        def _(step):
            k = 2 * step
            multiply((first, end, k + 1), 1)
            rest((first, end, k), 0)
            multiply((first, end, jnp.minimum(k + 2, len(blocks) - 1)), 0)
            rest((first, end, k + 1), 1)

    else:
        multiply(blocks[0], 0)
        for index, block in enumerate(blocks):
            if index + 1 < len(blocks):
                multiply(blocks[index + 1], (index + 1) % 2)
            rest(block, index % 2)
    if last:
        span = lax.broadcasted_iota(jnp.int32, (SPANS, SH), 0).astype(F32)
        table = jnp.zeros((SPANS, SH), F32)
        for start in range(0, NI, SH):
            at = slice(start, start + SH)
            part = jnp.sum(excess[:, at], axis=0, keepdims=True)
            table = table + jnp.where(meta[2:3, at] == span, part, 0.0)
        table = jnp.concatenate([table, jnp.zeros((SH - SPANS, SH), F32)], axis=0)
        result = jnp.sum(jnp.transpose(table), axis=0, keepdims=True)
        score[...] = jnp.broadcast_to(result, score.shape)


def shape(rows, columns, kind):
    return jax.ShapeDtypeStruct((rows, columns), kind)


def call(body, args, outs, scratch, estimate, aliases={}, mib=20):
    return pl.pallas_call(
        body,
        out_shape=tuple(shape(*out) for out in outs),
        in_specs=[VM] * len(args),
        out_specs=(VM,) * len(outs),
        scratch_shapes=[pltpu.VMEM((rows, columns), kind) for rows, columns, kind in scratch],
        input_output_aliases=aliases,
        compiler_params=params(mib),
        cost_estimate=estimate,
    )(*args)


STATE = [
    (NT, NI, BF16),
    (8, NI, F32),
    (8, NI, F32),
    (NI, D, BF16),
    (NT, D, BF16),
    (NI, D, BF16),
    (NT, D, BF16),
]


def run_stage(stage, chunks, state):
    new, blocks = STAGES[stage]
    texts = max(end - first for first, end, _ in blocks) * SH
    pairs_done = sum((end - first) * SH * CH for first, end, _ in blocks)
    estimate = pl.CostEstimate(
        flops=4 * pairs_done * D, bytes_accessed=8 << 20, transcendentals=3 * pairs_done
    )
    last = stage == len(STAGES) - 1
    outs = STATE + ([(8, SH, F32)] if last else [])
    aliases = {len(chunks) + i: i for i in range(len(STATE))} if stage else {}
    scratch = [(texts, CH, F32)] * 4
    args = [*chunks, *(state if stage else [])]
    return call(functools.partial(stage_kernel, stage), args, outs, scratch, estimate, aliases)


def image_kernel(half, grad, txt, out):
    out[...] = lax.dot_general(
        grad[:, half * NT : (half + 1) * NT],
        txt[...],
        (((0,), (0,)), ((), ())),
        preferred_element_type=F32,
    ).astype(BF16)


def image_part(grad, txt, half):
    body = functools.partial(image_kernel, half)
    estimate = pl.CostEstimate(flops=2 * NT * NT * D, bytes_accessed=6 << 20, transcendentals=0)
    return call(body, [grad, txt], [(NT, D, BF16)], [], estimate)[0]


def pair_kernel(mine, other, *outs):
    for k, out in enumerate(outs):
        at = slice(k * SH, (k + 1) * SH)
        out[...] = (mine[at].astype(F32) + other[at].astype(F32)).astype(BF16)


def pair_sum(mine, other):
    estimate = pl.CostEstimate(flops=0, bytes_accessed=8 << 20, transcendentals=0)
    return call(pair_kernel, [mine, other], [(SH, D, BF16)] * 8, [], estimate)


def text_kernel(score, meta, grad, img, *rest):
    *outs, weighted = rest
    weight = jax.nn.sigmoid(SHARP * score[0:1, :] / GROUP)
    column = jnp.transpose(jnp.broadcast_to(weight, (SH, SH)))[0:SPANS]
    span = lax.broadcasted_iota(jnp.int32, (SPANS, SH), 0).astype(F32)
    for start in range(0, NI, SH):
        at = slice(start, start + SH)
        chosen = jnp.where(meta[2:3, at] == span, column, 0.0)
        factor = jnp.sum(chosen, axis=0, keepdims=True)
        factor = factor * jnp.where(meta[3:4, at] == 1.0, SCALE * SYNTH, SCALE)
        weighted[:, at] = (grad[:, at].astype(F32) * factor).astype(BF16)
    for first in (4, 0):
        rows = slice(first * SH, (first + 4) * SH)
        total = jnp.dot(weighted[rows], img[...], preferred_element_type=F32)
        for k in range(4):
            outs[first + k][...] = total[k * SH : (k + 1) * SH].astype(BF16)


def text_part(score, meta, grad, img):
    estimate = pl.CostEstimate(flops=2 * NT * NI * D, bytes_accessed=12 << 20, transcendentals=0)
    outs = [(SH, D, BF16)] * 8
    return call(text_kernel, [score, meta, grad, img], outs, [(NT, NI, BF16)], estimate, mib=24)


def add(*terms):
    return sum(t.astype(F32) for t in terms)


def cube_sum(chunks, kind, *earlier):
    own, X, Y, Z, XY, YZ, ZX, XYZ = chunks
    to_yz = swap(XYZ, "x", kind)
    to_x = [swap(XY, "y", kind), swap(ZX, "z", kind)]
    from_y = swap(after(Y, *earlier), "y", kind)
    X = after(X, to_yz)
    from_z = swap(Z, "z", kind)
    from_yz = swap(add(YZ, to_yz).astype(BF16), "yz", kind)
    from_x = swap(add(X, *to_x).astype(BF16), "x", kind)
    total = add(own, from_yz, from_z)
    rest = after((from_x, from_y), total)
    return add(total, *rest), (from_y, from_z)


def shards(img_learner, txt_learner, img_ref, txt_ref, partner, synthetic, span_ids):
    core = core_index()
    meta = jnp.stack([partner, synthetic, span_ids])
    others = [swap(v, "c") for v in (img_learner, txt_learner, img_ref, txt_ref)]
    mine = [
        jnp.where(core == 0, img_learner, txt_learner),
        jnp.where(core == 0, img_ref, txt_ref),
    ]
    own = payload(mine, others, meta, swap(meta, "c"))
    near = cube_near(own)
    state = run_stage(0, near + [swap(v, "c") for v in near], None)
    edges = cube_edges(*near[1:])
    corner = cube_corner(*edges)
    state = run_stage(1, edges + [swap(v, "c") for v in edges], state)
    other_corner = [swap(v, "c") for v in after(corner, state[1])]
    state = run_stage(2, [], state)
    *state, partial = run_stage(3, corner + other_corner, state)
    grad, _, meta, img, txt, _, _ = state

    score = partial + swap(partial, "c")
    score = score + swap(score, "x", 0)
    img_send = image_part(grad, after(txt, score), 1)
    score = after(score + swap(score, "x", 1), img_send)
    img_other = swap(after(img_send, score), "c")
    img_keep = image_part(grad, after(txt, score), 0)
    score = after(score + swap(score, "y", 0), img_keep)
    score = score + swap(score, "y", 1)
    img_chunks = pair_sum(img_keep, after(img_other, score))
    score = after(score + swap(score, "z", 0), img_chunks)
    score = score + swap(score, "z", 1)

    img_total, img_near = cube_sum(img_chunks, 0)
    txt_total, _ = cube_sum(text_part(score, meta, grad, img), 1, *img_near)
    txt_grad = txt_total.astype(BF16)

    span_weight = jax.nn.sigmoid(SHARP * score[0, :SPANS] / GROUP)
    table = span_ids[:, None] == jnp.arange(SPANS, dtype=jnp.int32)[None, :]
    row_weight = jnp.sum(jnp.where(table, span_weight[None, :], 0.0), axis=1, keepdims=True)
    row_weight = row_weight * jnp.where(synthetic == 1, SCALE * SYNTH, SCALE)[:, None]
    img_grad = (img_total * row_weight).astype(BF16)
    return img_grad, txt_grad, span_weight


def solution(mesh):
    placed = (
        P(("row", "col"), None),
        P(("col", "row"), None),
        P(("row", "col"), None),
        P(("col", "row"), None),
        P(("row", "col")),
        P(("row", "col")),
        P(("row", "col")),
    )
    return jax.shard_map(
        shards,
        mesh=mesh,
        in_specs=placed,
        out_specs=(P(("row", "col"), None), P(("col", "row"), None), P()),
        check_vma=False,
    )
```

```python
import functools

import jax
import jax.numpy as jnp
from jax import lax
from jax.experimental import pallas as pl
from jax.experimental.pallas import tpu as pltpu
from jax.sharding import PartitionSpec as P

SPANS = 64
D = 1152
SH = 128
CH = 2 * SH
NT = 8 * SH
NI = 8 * CH
META = 16
REFER = CH + META
ROWS = REFER + CH
GROUP = 256.0
SCALE = 10.0
SHIFT = -5.0
SHARP = 5.0
SYNTH = 0.5
LN2 = 0.6931471805599453
LOG2E = 1.4426950408889634
AXES = ("row", "col")
F32 = jnp.float32
BF16 = jnp.bfloat16
MIB = 1 << 20

FLIPS = ("", "x", "y", "z", "xy", "yz", "zx", "xyz")


def place(index):
    row, col = divmod(index, 16)
    return dict(z=row // 2, y=2 * (row % 2) + col // 8, x=(col // 2) % 4, c=col % 2)


def device(z, y, x, c):
    return (2 * z + y // 2) * 16 + 8 * (y % 2) + 2 * x + c


def pairs(axes, kind):
    out = []
    for index in range(128):
        at = place(index)
        k = at["c"] if kind == "mixed" else kind
        for axis in axes:
            if axis == "c":
                at["c"] ^= 1
            else:
                at[axis] = at[axis] ^ 1 if k == 0 else 3 - at[axis]
        out.append((index, device(**at)))
    return out


def swap(value, axes, kind=0):
    return lax.ppermute(value, AXES, pairs(axes, kind))


VM = pl.BlockSpec(memory_space=pltpu.VMEM)


def params(mib):
    return pltpu.CompilerParams(vmem_limit_bytes=mib * MIB)


def core_index():
    return lax.rem(lax.axis_index("col"), 2)


def payload_kernel(mine_l, mine_r, oimg_l, otxt_l, oimg_r, otxt_r, meta, ometa, out):
    core = core_index()
    for place, mine, images, texts in ((0, mine_l, oimg_l, otxt_l), (REFER, mine_r, oimg_r, otxt_r)):
        out[place : place + SH] = jnp.where(core == 0, mine[...], texts[...])
        out[place + SH : place + CH] = jnp.where(core == 0, images[...], mine[...])
    out[CH:REFER] = jnp.zeros((META, D), BF16)
    row = lax.broadcasted_iota(jnp.int32, (META, SH), 0)
    for side, ref in enumerate((meta, ometa)):
        partner, synth, span = (ref[i : i + 1, :] for i in range(3))
        block = jnp.where(row == 0, lax.shift_right_logical(partner, 7), 0)
        block = jnp.where(row == 1, partner & 127, block)
        block = jnp.where(row == 2, span, block)
        block = jnp.where(row == 3, synth, block)
        out[CH:REFER, side * SH : (side + 1) * SH] = block.astype(F32).astype(BF16)


def payload(mine, others, meta, other_meta):
    estimate = pl.CostEstimate(flops=0, bytes_accessed=1 << 21, transcendentals=0)
    args = [*mine, *others, meta, other_meta]
    return call(payload_kernel, args, [(ROWS, D, BF16)], [], estimate, mib=8)[0]


def after(value, *others):
    return lax.optimization_barrier((value, others))[0]


def cube_near(own):
    return [own] + [swap(own, axis, "mixed") for axis in "xyz"]


def cube_edges(X, Y, Z):
    return [swap(Y, "x", "mixed"), swap(Z, "y", "mixed"), swap(X, "z", "mixed")]


def halves_kernel(yz, zx, learn, refer):
    learn[...] = yz[:REFER]
    refer[...] = zx[REFER:]


def cube_corner(XY, YZ, ZX):
    estimate = pl.CostEstimate(flops=0, bytes_accessed=4 << 20, transcendentals=0)
    outs = [(REFER, D, BF16), (CH, D, BF16)]
    learn, refer = call(halves_kernel, [YZ, ZX], outs, [], estimate)
    return [swap(learn, "x", "mixed"), swap(refer, "y", "mixed")]


def text_base(k, core):
    row, col = lax.axis_index("row"), lax.axis_index("col")
    z, yh = row // 2, lax.rem(row, 2)
    yl, x = col // 8, lax.rem(col // 2, 4)
    y = 2 * yh + yl
    x = 3 - x if "x" in FLIPS[k] else x
    y = 3 - y if "y" in FLIPS[k] else y
    z = 3 - z if "z" in FLIPS[k] else z
    col = 8 * lax.rem(y, 2) + 2 * x + core
    row = 2 * z + y // 2
    return (col * 8 + row) * SH


HALF = slice(0, SH), slice(SH, CH)


def pick(core, g, d, base, rows, half):
    mine, other = HALF[half], HALF[1 - half]
    at = slice(base + mine.start, base + mine.stop), slice(base + other.start, base + other.stop)
    return jnp.where(core == 0, g[at[0], :], d[at[1], :]) if rows == "images" else jnp.where(
        core == 0, d[at[0], :], g[at[1], :]
    )


def lanes(k, h):
    if isinstance(k, int):
        return slice(h * NT + k * SH, h * NT + (k + 1) * SH)
    return pl.ds(pl.multiple_of(h * NT + k * SH, SH), SH)


def product(left, right):
    return lax.dot_general(left, right, (((1,), (1,)), ((), ())), preferred_element_type=F32)


STEP = 32


def fold(value):
    return (value[0:8] + value[8:16]) + (value[16:24] + value[24:32])


def fold_product(value):
    return (value[0:8] * value[8:16]) * (value[16:24] * value[24:32])


def inverse(value):
    guess = pltpu.reciprocal(value, approx=True)
    return guess * (2.0 - value * guess)


def activate(learn, refer, partner, bases, store):
    rows, width = learn.shape
    iota = lax.broadcasted_iota(jnp.int32, (STEP, width), 0).astype(F32)
    positive = jnp.zeros((8, width), F32)
    logs = jnp.zeros((8, width), F32)
    factors = None
    count = 0
    for start in range(0, rows, STEP):
        chunk, inner = divmod(start, SH)
        mask = (partner - (bases[chunk] + inner).astype(F32)) == iota

        def part(ref):
            value = ref[start : start + STEP, :] * (SCALE * LOG2E) + (SHIFT * LOG2E)
            value = jnp.where(mask, -value, value)
            small = jnp.exp2(-jnp.abs(value))
            return value, small, 1.0 + small

        value, small, one = part(learn)
        value_r, _, one_r = part(refer)
        positive = positive + fold(jnp.maximum(value, 0.0) - jnp.maximum(value_r, 0.0))
        terms = fold_product(one), fold_product(one_r)
        factors = terms if factors is None else (factors[0] * terms[0], factors[1] * terms[1])
        count += 4
        if count == 64 or start + STEP == rows:
            logs = logs + (jnp.log(factors[0]) - jnp.log(factors[1]))
            factors, count = None, 0
        sig = jnp.where(value >= 0, 1.0, small) * inverse(one)
        store(start, jnp.where(mask, -sig, sig).astype(BF16))
    return positive * LN2 + logs


STAGES = (
    ((0, 1, 2, 3), [(0, 4, k) for k in range(4)]),
    ((4, 5, 6), [(0, 7, k) for k in (4, 5, 6)]),
    ((), [(4, 7, k) for k in range(4)]),
    ((7,), [(0, 8, 7)] + [(7, 8, k) for k in range(7)]),
)


LOOPS = (True, False, True, False)


def stage_kernel(stage, *refs):
    new, blocks = STAGES[stage]
    refs = list(refs)
    last = stage == len(STAGES) - 1
    if last:
        gs, ds, refs = [(refs[0], refs[1])], [(refs[2], refs[3])], refs[4:]
    else:
        count = len(new)
        gs, ds, refs = [(v, v) for v in refs[:count]], [(v, v) for v in refs[count : 2 * count]], refs[2 * count :]
    if stage > 0:
        refs = refs[len(STATE) :]
    grad, excess, meta, img_l, txt_l, img_r, txt_r = refs[: len(STATE)]
    refs = refs[len(STATE) :]
    if last:
        score, refs = refs[0], refs[1:]
    logits = refs
    core = core_index()
    models = ((0, img_l, txt_l), (0 if last else REFER, img_r, txt_r))
    for k, g, d in zip(new, gs, ds):
        for model, (base, img, txt) in enumerate(models):
            txt[k * SH : (k + 1) * SH] = pick(core, g[model], d[model], base, "texts", 0)
            for h in range(2):
                img[lanes(k, h)] = pick(core, g[model], d[model], base, "images", h)
        for h in range(2):
            block = jnp.where(core == 0, g[0][CH:REFER, HALF[h]], d[0][CH:REFER, HALF[1 - h]])
            meta[:, lanes(k, h)] = block.astype(F32)[0:8]
    bases = [text_base(k, core) for k in range(8)]

    def multiply(block, slot):
        first, end, k = block
        for model, (_, img, txt) in enumerate(models):
            images = jnp.concatenate([img[lanes(k, h), :] for h in range(2)], axis=0)
            logits[2 * slot + model][0 : (end - first) * SH] = product(txt[first * SH : end * SH], images)

    def rest(block, slot):
        first, end, k = block

        def store(start, value):
            row = first * SH + start
            for h in range(2):
                grad[row : row + STEP, lanes(k, h)] = value[:, HALF[h]]

        both = [meta[0:1, lanes(k, h)] * 128.0 + meta[1:2, lanes(k, h)] for h in range(2)]
        rows = slice(0, (end - first) * SH)
        learn, refer = (logits[2 * slot + model].at[rows] for model in range(2))
        total = activate(learn, refer, jnp.concatenate(both, axis=1), bases[first:end], store)
        for h in range(2):
            if first == 0:
                excess[:, lanes(k, h)] = total[:, HALF[h]]
            else:
                excess[:, lanes(k, h)] += total[:, HALF[h]]

    if LOOPS[stage]:
        first, end, _ = blocks[0]
        multiply(blocks[0], 0)

        @pl.loop(0, len(blocks) // 2)
        def _(step):
            k = 2 * step
            multiply((first, end, k + 1), 1)
            rest((first, end, k), 0)
            multiply((first, end, jnp.minimum(k + 2, len(blocks) - 1)), 0)
            rest((first, end, k + 1), 1)

    else:
        multiply(blocks[0], 0)
        for index, block in enumerate(blocks):
            if index + 1 < len(blocks):
                multiply(blocks[index + 1], (index + 1) % 2)
            rest(block, index % 2)
    if last:
        span = lax.broadcasted_iota(jnp.int32, (SPANS, SH), 0).astype(F32)
        table = jnp.zeros((SPANS, SH), F32)
        for start in range(0, NI, SH):
            at = slice(start, start + SH)
            part = jnp.sum(excess[:, at], axis=0, keepdims=True)
            table = table + jnp.where(meta[2:3, at] == span, part, 0.0)
        table = jnp.concatenate([table, jnp.zeros((SH - SPANS, SH), F32)], axis=0)
        result = jnp.sum(jnp.transpose(table), axis=0, keepdims=True)
        score[...] = jnp.broadcast_to(result, score.shape)


def shape(rows, columns, kind):
    return jax.ShapeDtypeStruct((rows, columns), kind)


def call(body, args, outs, scratch, estimate, aliases={}, mib=20):
    return pl.pallas_call(
        body,
        out_shape=tuple(shape(*out) for out in outs),
        in_specs=[VM] * len(args),
        out_specs=(VM,) * len(outs),
        scratch_shapes=[pltpu.VMEM((rows, columns), kind) for rows, columns, kind in scratch],
        input_output_aliases=aliases,
        compiler_params=params(mib),
        cost_estimate=estimate,
    )(*args)


STATE = [
    (NT, NI, BF16),
    (8, NI, F32),
    (8, NI, F32),
    (NI, D, BF16),
    (NT, D, BF16),
    (NI, D, BF16),
    (NT, D, BF16),
]


def run_stage(stage, chunks, state):
    new, blocks = STAGES[stage]
    texts = max(end - first for first, end, _ in blocks) * SH
    pairs_done = sum((end - first) * SH * CH for first, end, _ in blocks)
    estimate = pl.CostEstimate(
        flops=4 * pairs_done * D, bytes_accessed=8 << 20, transcendentals=3 * pairs_done
    )
    last = stage == len(STAGES) - 1
    outs = STATE + ([(8, SH, F32)] if last else [])
    aliases = {len(chunks) + i: i for i in range(len(STATE))} if stage else {}
    scratch = [(texts, CH, F32)] * 4
    args = [*chunks, *(state if stage else [])]
    return call(functools.partial(stage_kernel, stage), args, outs, scratch, estimate, aliases)


def image_kernel(half, grad, txt, out):
    @pl.loop(0, NT // (2 * CH))
    def _(block):
        at = pl.ds(pl.multiple_of(half * NT + block * 2 * CH, CH), 2 * CH)
        rows = pl.ds(pl.multiple_of(block * 2 * CH, CH), 2 * CH)
        out[rows, :] = lax.dot_general(
            grad[:, at], txt[...], (((0,), (0,)), ((), ())), preferred_element_type=F32
        ).astype(BF16)


def image_part(grad, txt, half):
    body = functools.partial(image_kernel, half)
    estimate = pl.CostEstimate(flops=2 * NT * NT * D, bytes_accessed=6 << 20, transcendentals=0)
    return call(body, [grad, txt], [(NT, D, BF16)], [], estimate)[0]


def pair_kernel(mine, other, *outs):
    for k, out in enumerate(outs):
        at = slice(k * SH, (k + 1) * SH)
        out[...] = (mine[at].astype(F32) + other[at].astype(F32)).astype(BF16)


def pair_sum(mine, other):
    estimate = pl.CostEstimate(flops=0, bytes_accessed=8 << 20, transcendentals=0)
    return call(pair_kernel, [mine, other], [(SH, D, BF16)] * 8, [], estimate)


def text_kernel(score, meta, grad, img, *rest):
    *outs, weighted = rest
    weight = jax.nn.sigmoid(SHARP * score[0:1, :] / GROUP)
    column = jnp.transpose(jnp.broadcast_to(weight, (SH, SH)))[0:SPANS]
    span = lax.broadcasted_iota(jnp.int32, (SPANS, SH), 0).astype(F32)
    for start in range(0, NI, SH):
        at = slice(start, start + SH)
        chosen = jnp.where(meta[2:3, at] == span, column, 0.0)
        factor = jnp.sum(chosen, axis=0, keepdims=True)
        factor = factor * jnp.where(meta[3:4, at] == 1.0, SCALE * SYNTH, SCALE)
        weighted[:, at] = (grad[:, at].astype(F32) * factor).astype(BF16)
    for first in (4, 0):
        rows = slice(first * SH, (first + 4) * SH)
        total = jnp.dot(weighted[rows], img[...], preferred_element_type=F32)
        for k in range(4):
            outs[first + k][...] = total[k * SH : (k + 1) * SH].astype(BF16)


def text_part(score, meta, grad, img):
    estimate = pl.CostEstimate(flops=2 * NT * NI * D, bytes_accessed=12 << 20, transcendentals=0)
    outs = [(SH, D, BF16)] * 8
    return call(text_kernel, [score, meta, grad, img], outs, [(NT, NI, BF16)], estimate, mib=24)


def add(*terms):
    return sum(t.astype(F32) for t in terms)


def cube_sum(chunks, kind, *earlier):
    own, X, Y, Z, XY, YZ, ZX, XYZ = chunks
    to_yz = swap(XYZ, "x", kind)
    to_x = [swap(XY, "y", kind), swap(ZX, "z", kind)]
    from_y = swap(after(Y, *earlier), "y", kind)
    X = after(X, to_yz)
    if kind == 1:
        Z = after(Z, to_yz)
    from_z = swap(Z, "z", kind)
    from_yz = swap(add(YZ, to_yz).astype(BF16), "yz", kind)
    from_x = swap(add(X, *to_x).astype(BF16), "x", kind)
    total = add(own, from_yz, from_z)
    rest = after((from_x, from_y), total)
    return add(total, *rest), (from_y, from_z)


def shards(img_learner, txt_learner, img_ref, txt_ref, partner, synthetic, span_ids):
    core = core_index()
    meta = jnp.stack([partner, synthetic, span_ids])
    others = [swap(v, "c") for v in (img_learner, txt_learner, img_ref, txt_ref)]
    mine = [
        jnp.where(core == 0, img_learner, txt_learner),
        jnp.where(core == 0, img_ref, txt_ref),
    ]
    own = payload(mine, others, meta, swap(meta, "c"))
    near = cube_near(own)
    state = run_stage(0, near + [swap(v, "c") for v in near], None)
    edges = cube_edges(*near[1:])
    edges[1] = after(edges[1], state[1])
    corner = cube_corner(*edges)
    state = run_stage(1, edges + [swap(v, "c") for v in edges], state)
    other_corner = [swap(v, "c") for v in after(corner, state[1])]
    state = run_stage(2, [], state)
    *state, partial = run_stage(3, corner + other_corner, state)
    grad, _, meta, img, txt, _, _ = state

    score = partial + swap(partial, "c")
    score = score + swap(score, "x", 0)
    img_send = image_part(grad, after(txt, score), 1)
    score = after(score + swap(score, "x", 1), img_send)
    img_other = swap(after(img_send, score), "c")
    img_keep = image_part(grad, after(txt, score), 0)
    score = after(score + swap(score, "y", 0), img_keep)
    score = score + swap(score, "y", 1)
    img_chunks = pair_sum(img_keep, after(img_other, score))
    score = after(score + swap(score, "z", 0), img_chunks)
    score = score + swap(score, "z", 1)

    txt_chunks = text_part(score, meta, grad, img)
    img_total, img_near = cube_sum(img_chunks, 0, txt_chunks[0])
    txt_total, _ = cube_sum(txt_chunks, 1, img_near[1])
    txt_grad = txt_total.astype(BF16)

    span_weight = jax.nn.sigmoid(SHARP * score[0, :SPANS] / GROUP)
    table = span_ids[:, None] == jnp.arange(SPANS, dtype=jnp.int32)[None, :]
    row_weight = jnp.sum(jnp.where(table, span_weight[None, :], 0.0), axis=1, keepdims=True)
    row_weight = row_weight * jnp.where(synthetic == 1, SCALE * SYNTH, SCALE)[:, None]
    img_grad = (img_total * row_weight).astype(BF16)
    return img_grad, txt_grad, span_weight


def solution(mesh):
    placed = (
        P(("row", "col"), None),
        P(("col", "row"), None),
        P(("row", "col"), None),
        P(("col", "row"), None),
        P(("row", "col")),
        P(("row", "col")),
        P(("row", "col")),
    )
    return jax.shard_map(
        shards,
        mesh=mesh,
        in_specs=placed,
        out_specs=(P(("row", "col"), None), P(("col", "row"), None), P()),
        check_vma=False,
    )
```

```python
import functools

import jax
import jax.numpy as jnp
from jax import lax
from jax.experimental import pallas as pl
from jax.experimental.pallas import tpu as pltpu
from jax.sharding import PartitionSpec as P

SPANS = 64
D = 1152
SH = 128
CH = 2 * SH
NT = 8 * SH
NI = 8 * CH
META = 16
REFER = CH + META
ROWS = REFER + CH
GROUP = 256.0
SCALE = 10.0
SHIFT = -5.0
SHARP = 5.0
SYNTH = 0.5
LN2 = 0.6931471805599453
LOG2E = 1.4426950408889634
AXES = ("row", "col")
F32 = jnp.float32
BF16 = jnp.bfloat16
MIB = 1 << 20

FLIPS = ("", "x", "y", "z", "xy", "yz", "zx", "xyz")


def place(index):
    row, col = divmod(index, 16)
    return dict(z=row // 2, y=2 * (row % 2) + col // 8, x=(col // 2) % 4, c=col % 2)


def device(z, y, x, c):
    return (2 * z + y // 2) * 16 + 8 * (y % 2) + 2 * x + c


def pairs(axes, kind):
    out = []
    for index in range(128):
        at = place(index)
        k = at["c"] if kind == "mixed" else kind
        for axis in axes:
            if axis == "c":
                at["c"] ^= 1
            else:
                at[axis] = at[axis] ^ 1 if k == 0 else 3 - at[axis]
        out.append((index, device(**at)))
    return out


def swap(value, axes, kind=0):
    return lax.ppermute(value, AXES, pairs(axes, kind))


VM = pl.BlockSpec(memory_space=pltpu.VMEM)


def params(mib):
    return pltpu.CompilerParams(vmem_limit_bytes=mib * MIB)


def core_index():
    return lax.rem(lax.axis_index("col"), 2)


def payload_kernel(mine_l, mine_r, oimg_l, otxt_l, oimg_r, otxt_r, meta, ometa, out):
    core = core_index()
    for place, mine, images, texts in ((0, mine_l, oimg_l, otxt_l), (REFER, mine_r, oimg_r, otxt_r)):
        out[place : place + SH] = jnp.where(core == 0, mine[...], texts[...])
        out[place + SH : place + CH] = jnp.where(core == 0, images[...], mine[...])
    out[CH:REFER] = jnp.zeros((META, D), BF16)
    row = lax.broadcasted_iota(jnp.int32, (META, SH), 0)
    for side, ref in enumerate((meta, ometa)):
        partner, synth, span = (ref[i : i + 1, :] for i in range(3))
        block = jnp.where(row == 0, lax.shift_right_logical(partner, 7), 0)
        block = jnp.where(row == 1, partner & 127, block)
        block = jnp.where(row == 2, span, block)
        block = jnp.where(row == 3, synth, block)
        out[CH:REFER, side * SH : (side + 1) * SH] = block.astype(F32).astype(BF16)


def payload(mine, others, meta, other_meta):
    estimate = pl.CostEstimate(flops=0, bytes_accessed=1 << 21, transcendentals=0)
    args = [*mine, *others, meta, other_meta]
    return call(payload_kernel, args, [(ROWS, D, BF16)], [], estimate, mib=8)[0]


def after(value, *others):
    return lax.optimization_barrier((value, others))[0]


def cube_near(own):
    return [own] + [swap(own, axis, "mixed") for axis in "xyz"]


def cube_edges(X, Y, Z):
    return [swap(Y, "x", "mixed"), swap(Z, "y", "mixed"), swap(X, "z", "mixed")]


def halves_kernel(yz, zx, learn, refer):
    learn[...] = yz[:REFER]
    refer[...] = zx[REFER:]


def cube_corner(XY, YZ, ZX):
    estimate = pl.CostEstimate(flops=0, bytes_accessed=4 << 20, transcendentals=0)
    outs = [(REFER, D, BF16), (CH, D, BF16)]
    learn, refer = call(halves_kernel, [YZ, ZX], outs, [], estimate)
    return [swap(learn, "x", "mixed"), swap(refer, "y", "mixed")]


def text_base(k, core):
    row, col = lax.axis_index("row"), lax.axis_index("col")
    z, yh = row // 2, lax.rem(row, 2)
    yl, x = col // 8, lax.rem(col // 2, 4)
    y = 2 * yh + yl
    x = 3 - x if "x" in FLIPS[k] else x
    y = 3 - y if "y" in FLIPS[k] else y
    z = 3 - z if "z" in FLIPS[k] else z
    col = 8 * lax.rem(y, 2) + 2 * x + core
    row = 2 * z + y // 2
    return (col * 8 + row) * SH


HALF = slice(0, SH), slice(SH, CH)


def pick(core, g, d, base, rows, half):
    mine, other = HALF[half], HALF[1 - half]
    at = slice(base + mine.start, base + mine.stop), slice(base + other.start, base + other.stop)
    return jnp.where(core == 0, g[at[0], :], d[at[1], :]) if rows == "images" else jnp.where(
        core == 0, d[at[0], :], g[at[1], :]
    )


def lanes(k, h):
    if isinstance(k, int):
        return slice(h * NT + k * SH, h * NT + (k + 1) * SH)
    return pl.ds(pl.multiple_of(h * NT + k * SH, SH), SH)


def product(left, right):
    return lax.dot_general(left, right, (((1,), (1,)), ((), ())), preferred_element_type=F32)


STEP = 32


def fold(value):
    return (value[0:8] + value[8:16]) + (value[16:24] + value[24:32])


def fold_product(value):
    return (value[0:8] * value[8:16]) * (value[16:24] * value[24:32])


def inverse(value):
    guess = pltpu.reciprocal(value, approx=True)
    return guess * (2.0 - value * guess)


def activate(learn, refer, partner, bases, store):
    rows, width = learn.shape
    iota = lax.broadcasted_iota(jnp.int32, (STEP, width), 0).astype(F32)
    positive = jnp.zeros((8, width), F32)
    logs = jnp.zeros((8, width), F32)
    factors = None
    count = 0
    for start in range(0, rows, STEP):
        chunk, inner = divmod(start, SH)
        mask = (partner - (bases[chunk] + inner).astype(F32)) == iota

        def part(ref):
            value = ref[start : start + STEP, :] * (SCALE * LOG2E) + (SHIFT * LOG2E)
            value = jnp.where(mask, -value, value)
            small = jnp.exp2(-jnp.abs(value))
            return value, small, 1.0 + small

        value, small, one = part(learn)
        value_r, _, one_r = part(refer)
        positive = positive + fold(jnp.maximum(value, 0.0) - jnp.maximum(value_r, 0.0))
        terms = fold_product(one), fold_product(one_r)
        factors = terms if factors is None else (factors[0] * terms[0], factors[1] * terms[1])
        count += 4
        if count == 64 or start + STEP == rows:
            logs = logs + (jnp.log(factors[0]) - jnp.log(factors[1]))
            factors, count = None, 0
        sig = jnp.where(value >= 0, 1.0, small) * inverse(one)
        store(start, jnp.where(mask, -sig, sig).astype(BF16))
    return positive * LN2 + logs


STAGES = (
    ((0, 1, 2, 3), [(0, 4, k) for k in range(4)]),
    ((4, 5, 6), [(0, 7, k) for k in (4, 5, 6)]),
    ((), [(4, 7, k) for k in range(4)]),
    ((7,), [(0, 8, 7)] + [(7, 8, k) for k in range(7)]),
)


LOOPS = (True, False, False, False)


def stage_kernel(stage, *refs):
    new, blocks = STAGES[stage]
    refs = list(refs)
    last = stage == len(STAGES) - 1
    if last:
        gs, ds, refs = [(refs[0], refs[1])], [(refs[2], refs[3])], refs[4:]
    else:
        count = len(new)
        gs, ds, refs = [(v, v) for v in refs[:count]], [(v, v) for v in refs[count : 2 * count]], refs[2 * count :]
    if stage > 0:
        refs = refs[len(STATE) :]
    grad, excess, meta, img_l, txt_l, img_r, txt_r = refs[: len(STATE)]
    refs = refs[len(STATE) :]
    if last:
        score, refs = refs[0], refs[1:]
    logits = refs
    core = core_index()
    models = ((0, img_l, txt_l), (0 if last else REFER, img_r, txt_r))
    for k, g, d in zip(new, gs, ds):
        for model, (base, img, txt) in enumerate(models):
            txt[k * SH : (k + 1) * SH] = pick(core, g[model], d[model], base, "texts", 0)
            for h in range(2):
                img[lanes(k, h)] = pick(core, g[model], d[model], base, "images", h)
        for h in range(2):
            block = jnp.where(core == 0, g[0][CH:REFER, HALF[h]], d[0][CH:REFER, HALF[1 - h]])
            meta[:, lanes(k, h)] = block.astype(F32)[0:8]
    bases = [text_base(k, core) for k in range(8)]

    def multiply(block, slot):
        first, end, k = block
        for model, (_, img, txt) in enumerate(models):
            images = jnp.concatenate([img[lanes(k, h), :] for h in range(2)], axis=0)
            logits[2 * slot + model][0 : (end - first) * SH] = product(txt[first * SH : end * SH], images)

    def rest(block, slot):
        first, end, k = block

        def store(start, value):
            row = first * SH + start
            for h in range(2):
                grad[row : row + STEP, lanes(k, h)] = value[:, HALF[h]]

        both = [meta[0:1, lanes(k, h)] * 128.0 + meta[1:2, lanes(k, h)] for h in range(2)]
        rows = slice(0, (end - first) * SH)
        learn, refer = (logits[2 * slot + model].at[rows] for model in range(2))
        total = activate(learn, refer, jnp.concatenate(both, axis=1), bases[first:end], store)
        for h in range(2):
            if first == 0:
                excess[:, lanes(k, h)] = total[:, HALF[h]]
            else:
                excess[:, lanes(k, h)] += total[:, HALF[h]]

    if LOOPS[stage]:
        first, end, _ = blocks[0]
        multiply(blocks[0], 0)

        @pl.loop(0, len(blocks) // 2)
        def _(step):
            k = 2 * step
            multiply((first, end, k + 1), 1)
            rest((first, end, k), 0)
            multiply((first, end, jnp.minimum(k + 2, len(blocks) - 1)), 0)
            rest((first, end, k + 1), 1)

    else:
        multiply(blocks[0], 0)
        for index, block in enumerate(blocks):
            if index + 1 < len(blocks):
                multiply(blocks[index + 1], (index + 1) % 2)
            rest(block, index % 2)
    if last:
        span = lax.broadcasted_iota(jnp.int32, (SPANS, SH), 0).astype(F32)
        table = jnp.zeros((SPANS, SH), F32)
        for start in range(0, NI, SH):
            at = slice(start, start + SH)
            part = jnp.sum(excess[:, at], axis=0, keepdims=True)
            table = table + jnp.where(meta[2:3, at] == span, part, 0.0)
        table = jnp.concatenate([table, jnp.zeros((SH - SPANS, SH), F32)], axis=0)
        result = jnp.sum(jnp.transpose(table), axis=0, keepdims=True)
        score[...] = jnp.broadcast_to(result, score.shape)


def shape(rows, columns, kind):
    return jax.ShapeDtypeStruct((rows, columns), kind)


def call(body, args, outs, scratch, estimate, aliases={}, mib=20):
    return pl.pallas_call(
        body,
        out_shape=tuple(shape(*out) for out in outs),
        in_specs=[VM] * len(args),
        out_specs=(VM,) * len(outs),
        scratch_shapes=[pltpu.VMEM((rows, columns), kind) for rows, columns, kind in scratch],
        input_output_aliases=aliases,
        compiler_params=params(mib),
        cost_estimate=estimate,
    )(*args)


STATE = [
    (NT, NI, BF16),
    (8, NI, F32),
    (8, NI, F32),
    (NI, D, BF16),
    (NT, D, BF16),
    (NI, D, BF16),
    (NT, D, BF16),
]


def run_stage(stage, chunks, state):
    new, blocks = STAGES[stage]
    texts = max(end - first for first, end, _ in blocks) * SH
    pairs_done = sum((end - first) * SH * CH for first, end, _ in blocks)
    estimate = pl.CostEstimate(
        flops=4 * pairs_done * D, bytes_accessed=8 << 20, transcendentals=3 * pairs_done
    )
    last = stage == len(STAGES) - 1
    outs = STATE + ([(8, SH, F32)] if last else [])
    aliases = {len(chunks) + i: i for i in range(len(STATE))} if stage else {}
    scratch = [(texts, CH, F32)] * 4
    args = [*chunks, *(state if stage else [])]
    return call(functools.partial(stage_kernel, stage), args, outs, scratch, estimate, aliases)


def image_kernel(half, grad, txt, out):
    @pl.loop(0, NT // (2 * CH))
    def _(block):
        at = pl.ds(pl.multiple_of(half * NT + block * 2 * CH, CH), 2 * CH)
        rows = pl.ds(pl.multiple_of(block * 2 * CH, CH), 2 * CH)
        out[rows, :] = lax.dot_general(
            grad[:, at], txt[...], (((0,), (0,)), ((), ())), preferred_element_type=F32
        ).astype(BF16)


def image_part(grad, txt, half):
    body = functools.partial(image_kernel, half)
    estimate = pl.CostEstimate(flops=2 * NT * NT * D, bytes_accessed=6 << 20, transcendentals=0)
    return call(body, [grad, txt], [(NT, D, BF16)], [], estimate)[0]


def pair_kernel(mine, other, *outs):
    for k, out in enumerate(outs):
        at = slice(k * SH, (k + 1) * SH)
        out[...] = (mine[at].astype(F32) + other[at].astype(F32)).astype(BF16)


def pair_sum(mine, other):
    estimate = pl.CostEstimate(flops=0, bytes_accessed=8 << 20, transcendentals=0)
    return call(pair_kernel, [mine, other], [(SH, D, BF16)] * 8, [], estimate)


def text_kernel(score, meta, grad, img, *rest):
    *outs, weighted = rest
    weight = jax.nn.sigmoid(SHARP * score[0:1, :] / GROUP)
    column = jnp.transpose(jnp.broadcast_to(weight, (SH, SH)))[0:SPANS]
    span = lax.broadcasted_iota(jnp.int32, (SPANS, SH), 0).astype(F32)
    for start in range(0, NI, SH):
        at = slice(start, start + SH)
        chosen = jnp.where(meta[2:3, at] == span, column, 0.0)
        factor = jnp.sum(chosen, axis=0, keepdims=True)
        factor = factor * jnp.where(meta[3:4, at] == 1.0, SCALE * SYNTH, SCALE)
        weighted[:, at] = (grad[:, at].astype(F32) * factor).astype(BF16)
    for first in (4, 0):
        rows = slice(first * SH, (first + 4) * SH)
        total = jnp.dot(weighted[rows], img[...], preferred_element_type=F32)
        for k in range(4):
            outs[first + k][...] = total[k * SH : (k + 1) * SH].astype(BF16)


def text_part(score, meta, grad, img):
    estimate = pl.CostEstimate(flops=2 * NT * NI * D, bytes_accessed=12 << 20, transcendentals=0)
    outs = [(SH, D, BF16)] * 8
    return call(text_kernel, [score, meta, grad, img], outs, [(NT, NI, BF16)], estimate, mib=24)


def add(*terms):
    return sum(t.astype(F32) for t in terms)


def cube_sum(chunks, kind, *earlier):
    own, X, Y, Z, XY, YZ, ZX, XYZ = chunks
    to_yz = swap(XYZ, "x", kind)
    to_x = [swap(XY, "y", kind), swap(ZX, "z", kind)]
    from_y = swap(after(Y, *earlier), "y", kind)
    X = after(X, to_yz)
    if kind == 1:
        Z = after(Z, to_yz)
    from_z = swap(Z, "z", kind)
    from_yz = swap(add(YZ, to_yz).astype(BF16), "yz", kind)
    from_x = swap(add(X, *to_x).astype(BF16), "x", kind)
    total = add(own, from_yz, from_z)
    rest = after((from_x, from_y), total)
    return add(total, *rest), (from_y, from_z)


def shards(img_learner, txt_learner, img_ref, txt_ref, partner, synthetic, span_ids):
    core = core_index()
    meta = jnp.stack([partner, synthetic, span_ids])
    others = [swap(v, "c") for v in (img_learner, txt_learner, img_ref, txt_ref)]
    mine = [
        jnp.where(core == 0, img_learner, txt_learner),
        jnp.where(core == 0, img_ref, txt_ref),
    ]
    own = payload(mine, others, meta, swap(meta, "c"))
    near = cube_near(own)
    state = run_stage(0, near + [swap(v, "c") for v in near], None)
    edges = cube_edges(*near[1:])
    edges[1] = after(edges[1], state[1])
    corner = cube_corner(*edges)
    state = run_stage(1, edges + [swap(v, "c") for v in edges], state)
    other_corner = [swap(v, "c") for v in after(corner, state[1])]
    state = run_stage(2, [], state)
    *state, partial = run_stage(3, corner + other_corner, state)
    grad, _, meta, img, txt, _, _ = state

    score = partial + swap(partial, "c")
    score = score + swap(score, "x", 0)
    img_send = image_part(grad, after(txt, score), 1)
    score = after(score + swap(score, "x", 1), img_send)
    img_other = swap(after(img_send, score), "c")
    img_keep = image_part(grad, after(txt, score), 0)
    score = after(score + swap(score, "y", 0), img_keep)
    score = score + swap(score, "y", 1)
    img_chunks = pair_sum(img_keep, after(img_other, score))
    score = after(score + swap(score, "z", 0), img_chunks)
    score = score + swap(score, "z", 1)

    txt_chunks = text_part(score, meta, grad, img)
    img_total, img_near = cube_sum(img_chunks, 0, txt_chunks[0])
    txt_total, _ = cube_sum(txt_chunks, 1, img_near[1])
    txt_grad = txt_total.astype(BF16)

    span_weight = jax.nn.sigmoid(SHARP * score[0, :SPANS] / GROUP)
    table = span_ids[:, None] == jnp.arange(SPANS, dtype=jnp.int32)[None, :]
    row_weight = jnp.sum(jnp.where(table, span_weight[None, :], 0.0), axis=1, keepdims=True)
    row_weight = row_weight * jnp.where(synthetic == 1, SCALE * SYNTH, SCALE)[:, None]
    img_grad = (img_total * row_weight).astype(BF16)
    return img_grad, txt_grad, span_weight


def solution(mesh):
    placed = (
        P(("row", "col"), None),
        P(("col", "row"), None),
        P(("row", "col"), None),
        P(("col", "row"), None),
        P(("row", "col")),
        P(("row", "col")),
        P(("row", "col")),
    )
    return jax.shard_map(
        shards,
        mesh=mesh,
        in_specs=placed,
        out_specs=(P(("row", "col"), None), P(("col", "row"), None), P()),
        check_vma=False,
    )
```
